128 devices in a mesh: replica: 8 (over z, x_hi), fsdp: 16 (over y, x_lo, core).
Axes of the slice: x: 4 (x_hi: 2, x_lo: 2; x = x_hi * 2 + x_lo), y: 4, z: 4, core: 2. Of those that a mesh axis runs over, the one named last changes fastest.
Arguments:
- attention: bfloat16 [8, 8192, 2048], P('replica', 'fsdp'), may hold values from -6 to 6
- upstream: bfloat16 [8, 8192, 4608], P('replica', 'fsdp'), may hold values from -6 to 6
- step_index: int32 [], replicated, may hold values from 0 to 63
- weight: float32 [8, 4608, 2048], P('replica', 'fsdp'), may hold values from -0.125 to 0.125
- weight_momentum: float32 [8, 4608, 2048], P('replica', 'fsdp'), may hold values from -6 to 6
- weight_variance: float32 [8, 4608, 2048], P('replica', 'fsdp'), may hold values from 1 to 100
- norm_gain: float32 [8, 4608], P('replica', 'fsdp'), may hold values from 0.5 to 1.5
- gain_momentum: float32 [8, 4608], P('replica', 'fsdp'), may hold values from -6 to 6
- gain_variance: float32 [8, 4608], P('replica', 'fsdp'), may hold values from 1 to 100
Outputs:
- grad_input: bfloat16 [8, 8192, 2048], P('replica', 'fsdp')
- new_weight: float32 [8, 4608, 2048], P('replica', 'fsdp')
- new_weight_momentum: float32 [8, 4608, 2048], P('replica', 'fsdp')
- new_weight_variance: float32 [8, 4608, 2048], P('replica', 'fsdp')
- new_gain: float32 [8, 4608], P('replica', 'fsdp')
- new_gain_momentum: float32 [8, 4608], P('replica', 'fsdp')
- new_gain_variance: float32 [8, 4608], P('replica', 'fsdp')
The draws below stay inside these ranges and needn't reach their ends.
All inputs are finite; a program needn't handle non-finite values.
Results may differ from the reference program's by a relative error of at most 0.02.
Values may be sent and summed in bfloat16 or wider, within the bound.
No kernel may reach another device: no remote copies, remote signals or barrier semaphores. Data moves between devices by JAX's collectives and lax.ppermute only.
A program may use at most 192 MiB of HBM per device.

```python
import math
import jax
import jax.numpy as jnp
from jax import lax

D = 4608
TOK_DEV = 512
HQ = 2048
GROUP_TOK = 8192
N_REPLICA = 8
N_FSDP = 16


def shard_levels(own_key, extent, cuts, least, high):
    factor_of, own = 1.0, jax.random.fold_in(own_key, 6)
    for dim, blocks in cuts:
        heights = jnp.exp(jax.random.uniform(jax.random.fold_in(own, dim), (blocks,), jnp.float32, least / len(cuts), high / len(cuts)))
        factor_of = factor_of * jnp.repeat(heights, extent[dim] // blocks).reshape([-1 if axis == dim else 1 for axis in range(len(extent))])
    return factor_of


def normal_values(stream_key, dims, scale, bound, shards=(), kind=jnp.bfloat16):
    entries = scale * jax.random.normal(stream_key, dims, jnp.float32)
    if shards:
        entries = entries * shard_levels(stream_key, dims, shards, -0.22, 0.18)
    return jnp.clip(entries, -bound, bound).astype(kind)


def setup_inputs(seed: int = 0) -> dict:
    seeds = jax.random.split(jax.random.key(seed), 10)
    return {
        "attention": normal_values(seeds[0], (N_REPLICA, GROUP_TOK, HQ), 1.0, 6.0, ((0, 8), (1, 16))),
        "upstream": normal_values(seeds[1], (N_REPLICA, GROUP_TOK, D), 1.0, 6.0, ((0, 8), (1, 16))),
        "step_index": jax.random.randint(seeds[2], (), 0, 64).astype(jnp.int32),
        "weight": normal_values(seeds[3], (N_REPLICA, D, HQ), HQ ** -0.5, 0.125, ((0, 8), (1, 16)), jnp.float32),
        "weight_momentum": normal_values(seeds[4], (N_REPLICA, D, HQ), 1.0, 6.0, ((0, 8), (1, 16)), jnp.float32),
        "weight_variance": jnp.clip(jnp.exp(math.log(100.0) - 4.6051702 * jax.random.uniform(seeds[5], (N_REPLICA, D, HQ), jnp.float32) ** shard_levels(seeds[5], (N_REPLICA, D, HQ), ((0, 8), (1, 16)), -0.2, 0.2)), 1.0, 100.0),
        "norm_gain": jnp.clip(1.0 + 0.1 * jax.random.normal(seeds[6], (N_REPLICA, D), jnp.float32), 0.5, 1.5),
        "gain_momentum": normal_values(seeds[7], (N_REPLICA, D), 1.0, 6.0, ((0, 8), (1, 16)), jnp.float32),
        "gain_variance": jnp.clip(jnp.exp(math.log(100.0) - 4.6051702 * jax.random.uniform(seeds[8], (N_REPLICA, D), jnp.float32) ** shard_levels(seeds[8], (N_REPLICA, D), ((0, 8), (1, 16)), -0.2, 0.2)), 1.0, 100.0),
    }


learn_rate = 0.001
beta_first = 0.9
beta_second = 0.999
decay_rate = 0.1
adam_eps = 1e-08
norm_eps = 1e-06

def group_grads(attention, upstream, weight, norm_gain):
    weight_low = weight.astype(jnp.bfloat16)
    gain_low = lax.optimization_barrier(norm_gain.astype(jnp.bfloat16)).astype(jnp.float32)
    output = jnp.dot(attention, weight_low.T, preferred_element_type=jnp.float32)
    inverse_rms = lax.rsqrt(lax.optimization_barrier(jnp.mean(output * output, -1, keepdims=True)) + norm_eps)
    normed = output * inverse_rms
    scaled = upstream.astype(jnp.float32) * gain_low
    grad_normin = (inverse_rms * (scaled - normed * lax.optimization_barrier(jnp.mean(scaled * normed, -1, keepdims=True)))).astype(jnp.bfloat16)
    grad_input = jnp.dot(grad_normin, weight_low, preferred_element_type=jnp.float32).astype(jnp.bfloat16)
    blocks_grad = grad_normin.reshape(N_FSDP, TOK_DEV, D)
    blocks_attn = attention.reshape(N_FSDP, TOK_DEV, HQ)

    def accumulate(total, pair):
        term = lax.dot_general(pair[0], pair[1], (((0,), (0,)), ((), ())), preferred_element_type=jnp.float32)
        return (total + lax.optimization_barrier(term.astype(jnp.bfloat16)).astype(jnp.float32), None)
    grad_weight, _ = lax.scan(accumulate, jnp.zeros((D, HQ), jnp.float32), (blocks_grad, blocks_attn))
    grad_gain = lax.optimization_barrier(jnp.sum(upstream.astype(jnp.float32) * normed, 0))
    return (grad_input, grad_weight, grad_gain)

def adamw(params, grads, momentum, variance, step_index):
    counted = (step_index + 1).astype(jnp.float32)
    new_momentum = beta_first * momentum + (1.0 - beta_first) * grads
    new_variance = beta_second * variance + (1.0 - beta_second) * grads * grads
    first_hat = new_momentum / (1.0 - jnp.power(jnp.float32(beta_first), counted))
    second_hat = new_variance / (1.0 - jnp.power(jnp.float32(beta_second), counted))
    update = learn_rate * (first_hat / (jnp.sqrt(second_hat) + adam_eps) + decay_rate * params)
    return (params - update, new_momentum, new_variance)

def reference(attention, upstream, step_index, weight, weight_momentum, weight_variance, norm_gain, gain_momentum, gain_variance):
    grad_input, grad_weight, grad_gain = lax.map(lambda items: group_grads(*items), (attention, upstream, weight, norm_gain))
    local_weight, new_weight_momentum, new_weight_variance = adamw(weight, grad_weight, weight_momentum, weight_variance, step_index)
    local_gain, new_gain_momentum, new_gain_variance = adamw(norm_gain, grad_gain, gain_momentum, gain_variance, step_index)
    levels = N_REPLICA.bit_length() - 1
    partner_bit = (step_index % levels).astype(jnp.int32)
    partner = jnp.bitwise_xor(jnp.arange(N_REPLICA, dtype=jnp.int32), jnp.left_shift(jnp.int32(1), partner_bit))
    new_weight = 0.5 * (local_weight + local_weight[partner])
    new_gain = 0.5 * (local_gain + local_gain[partner])
    return (grad_input, new_weight, new_weight_momentum, new_weight_variance, new_gain, new_gain_momentum, new_gain_variance)
```

```python
from functools import partial

import jax
import jax.numpy as jnp
from jax import lax
from jax.sharding import PartitionSpec as P

learn_rate = 0.001
beta_first = 0.9
beta_second = 0.999
decay_rate = 0.1
adam_eps = 1e-08
norm_eps = 1e-06

NY, NX, NC = 4, 2, 2
PIECES = 2


def place(y, x, core):
    return ((y % NY) * NX + x % NX) * NC + core % NC


def route(dy, dx, dcore):
    return [
        (place(y, x, core), place(y + dy, x + dx, core + dcore))
        for y in range(NY)
        for x in range(NX)
        for core in range(NC)
    ]


def move(block, dy=0, dx=0, dcore=0):
    return lax.ppermute(block, "fsdp", route(dy, dx, dcore))


def swapped(block, bit):
    count = lax.axis_size("replica")
    return lax.ppermute(block, "replica", [(low, low ^ (1 << bit)) for low in range(count)])


def adam_update(params, grads, momentum, variance, step_index):
    counted = (step_index + 1).astype(jnp.float32)
    new_momentum = beta_first * momentum + (1.0 - beta_first) * grads
    new_variance = beta_second * variance + (1.0 - beta_second) * grads * grads
    first_hat = new_momentum / (1.0 - jnp.power(jnp.float32(beta_first), counted))
    second_hat = new_variance / (1.0 - jnp.power(jnp.float32(beta_second), counted))
    update = learn_rate * (first_hat / (jnp.sqrt(second_hat) + adam_eps) + decay_rate * params)
    return (params - update, new_momentum, new_variance)


def gather_rows(own):
    half = own.shape[0] // 2
    across = move(own, dx=1)
    below = move(own, dy=1)
    above = move(own, dy=-1)
    far_top = move(below[:half], dy=1)
    far_bottom = move(above[half:], dy=-1)
    across_below = move(across, dy=1)
    across_above = move(across, dy=-1)
    far = jnp.concatenate([far_top, far_bottom])
    across_far = move(far, dx=1)
    return [own, across, below, above, across_below, across_above, far, across_far]


def gather_gain(own):
    pair = jnp.concatenate([own, move(own, dx=1)])
    below = move(pair, dy=1)
    above = move(pair, dy=-1)
    far = move(below, dy=1)
    return [pair[0], pair[1], below[0], above[0], below[1], above[1], far[0], far[1]]


def scatter_gain(parts):
    own, across, below, above, across_below, across_above, far, across_far = parts
    arrived = move(jnp.stack([far, across_far]), dy=1)
    up = move(jnp.stack([above, across_above]) + arrived, dy=1)
    down = move(jnp.stack([below, across_below]), dy=-1)
    pair = jnp.stack([own, across]) + up + down
    return pair[0] + move(pair[1], dx=1)


def body(
    level,
    attention,
    upstream,
    step_index,
    weight,
    weight_momentum,
    weight_variance,
    norm_gain,
    gain_momentum,
    gain_variance,
):
    rows, features = weight.shape[1:]
    tokens, width = upstream.shape[1:]
    low = jnp.bfloat16
    index = lax.axis_index("fsdp")
    core = index % NC
    x = index // NC % NX
    y = index // (NC * NX)
    offsets = [(0, 0), (0, 1), (-1, 0), (1, 0), (-1, 1), (1, 1), (2, 0), (2, 1)]

    blocks = gather_rows(weight[0].astype(low))
    gains = gather_gain(norm_gain.astype(low).astype(jnp.float32))

    attn = jnp.concatenate([attention[0], move(attention[0], dcore=1)])
    up_rows = upstream[0].T.reshape(width // rows, rows, tokens)
    mine = []
    theirs = []
    for dy, dx in offsets:
        at = place(y + dy, x + dx, 0)
        mine.append(lax.dynamic_index_in_dim(up_rows, at + core, 0, False))
        theirs.append(lax.dynamic_index_in_dim(up_rows, at + 1 - core, 0, False))
    given = move(jnp.stack(theirs), dcore=1)
    ups = [jnp.concatenate([own, given[k]], 1) for k, own in enumerate(mine)]

    outputs = []
    square = jnp.zeros((NC * tokens,), jnp.float32)
    cross = jnp.zeros((NC * tokens,), jnp.float32)
    for block, gain, up in zip(blocks, gains, ups):
        out = lax.dot_general(
            block, attn, (((1,), (1,)), ((), ())), preferred_element_type=jnp.float32
        )
        square = square + jnp.sum(out * out, 0)
        cross = cross + jnp.sum(out * (up.astype(jnp.float32) * gain[:, None]), 0)
        outputs.append(out)
    sums = jnp.stack([square, cross])
    other = move(sums, dcore=1)
    sums = sums + jnp.concatenate([other[:, tokens:], other[:, :tokens]], 1)
    inverse_rms = lax.rsqrt(sums[0] / width + norm_eps)
    slope = sums[1] / width * inverse_rms * inverse_rms
    grads = []
    gain_parts = []
    for out, gain, up in zip(outputs, gains, ups):
        up = up.astype(jnp.float32)
        grads.append((inverse_rms * (up * gain[:, None] - out * slope)).astype(low))
        gain_parts.append(jnp.sum(up * (out * inverse_rms), 1))

    def partial_grad(k, columns=slice(None)):
        return jnp.dot(grads[k], attn[:, columns], preferred_element_type=jnp.float32)

    half = rows // 2
    across_far = move(partial_grad(7).astype(low), dx=1)
    from_above = move(partial_grad(4).astype(low), dy=-1)
    from_below = move(partial_grad(5).astype(low), dy=1)
    far = (partial_grad(6) + across_far.astype(jnp.float32)).astype(low)
    far_top = move(far[:half], dy=-1)
    far_bottom = move(far[half:], dy=1)
    across = (
        partial_grad(1) + from_above.astype(jnp.float32) + from_below.astype(jnp.float32)
    ).astype(low)
    nothing = jnp.zeros((half, features), low)
    below = (
        partial_grad(2) + jnp.concatenate([far_top, nothing]).astype(jnp.float32)
    ).astype(low)
    above = (
        partial_grad(3) + jnp.concatenate([nothing, far_bottom]).astype(jnp.float32)
    ).astype(low)

    span = features // PIECES
    results = []
    for piece in range(PIECES):
        columns = slice(piece * span, (piece + 1) * span)
        side = move(across[:, columns], dx=1)
        down = move(below[:, columns], dy=-1)
        up = move(above[:, columns], dy=1)
        grad = (
            partial_grad(0, columns)
            + side.astype(jnp.float32)
            + down.astype(jnp.float32)
            + up.astype(jnp.float32)
        )
        local, momentum, variance = adam_update(
            weight[0, :, columns],
            grad,
            weight_momentum[0, :, columns],
            weight_variance[0, :, columns],
            step_index,
        )
        peer = swapped(local.astype(low), level)
        results.append((0.5 * (local + peer.astype(jnp.float32)), momentum, variance))
    new_weight, new_weight_momentum, new_weight_variance = [
        jnp.concatenate(parts, 1)[None] for parts in zip(*results)
    ]

    grad_gain = scatter_gain(gain_parts)
    local_gain, new_gain_momentum, new_gain_variance = adam_update(
        norm_gain, grad_gain[None], gain_momentum, gain_variance, step_index
    )
    new_gain = 0.5 * (local_gain + swapped(local_gain, level))

    both = lax.dot_general(
        jnp.concatenate(grads),
        jnp.concatenate(blocks),
        (((0,), (0,)), ((), ())),
        preferred_element_type=jnp.float32,
    )
    grad_input = (
        both[:tokens] + move(both[tokens:].astype(low), dcore=1).astype(jnp.float32)
    ).astype(low)
    return (
        grad_input[None],
        new_weight,
        new_weight_momentum,
        new_weight_variance,
        new_gain,
        new_gain_momentum,
        new_gain_variance,
    )


def shards(attention, upstream, step_index, *params):
    levels = lax.axis_size("replica").bit_length() - 1
    return lax.switch(
        step_index % levels,
        [partial(body, level) for level in range(levels)],
        attention,
        upstream,
        step_index,
        *params,
    )


def solution(mesh):
    block = P("replica", "fsdp", None)
    vector = P("replica", "fsdp")
    return jax.shard_map(
        shards,
        mesh=mesh,
        in_specs=(block, block, P(), block, block, block, vector, vector, vector),
        out_specs=(block, block, block, block, vector, vector, vector),
        check_vma=False,
    )
```

```python
from functools import partial

import jax
import jax.numpy as jnp
from jax import lax
from jax.experimental import pallas as pl
from jax.experimental.pallas import tpu as pltpu
from jax.sharding import PartitionSpec as P

learn_rate = 0.001
beta_first = 0.9
beta_second = 0.999
decay_rate = 0.1
adam_eps = 1e-08
norm_eps = 1e-06

NY, NX, NC = 4, 2, 2
CUT = 768
GAIN_ROWS = 8
EXTRA_BYTES = 0
NO_COST = pl.CostEstimate(flops=0, bytes_accessed=0, transcendentals=0)
SMALL_COST = pl.CostEstimate(flops=1_200_000_000, bytes_accessed=0, transcendentals=0)


def place(y, x, core):
    return ((y % NY) * NX + x % NX) * NC + core % NC


def route(dy, dx, dcore):
    return [
        (place(y, x, core), place(y + dy, x + dx, core + dcore))
        for y in range(NY)
        for x in range(NX)
        for core in range(NC)
    ]


def move(block, dy=0, dx=0, dcore=0):
    return lax.ppermute(block, "fsdp", route(dy, dx, dcore))


def swapped(values, step_index):
    count = lax.axis_size("replica")
    levels = count.bit_length() - 1

    def swap(level, *parts):
        pairs = [(low, low ^ (1 << level)) for low in range(count)]
        return tuple(lax.ppermute(part, "replica", pairs) for part in parts)

    return lax.switch(
        step_index % levels, [partial(swap, level) for level in range(levels)], *values
    )


def adam_update(params, grads, momentum, variance, step_index):
    counted = (step_index + 1).astype(jnp.float32)
    new_momentum = beta_first * momentum + (1.0 - beta_first) * grads
    new_variance = beta_second * variance + (1.0 - beta_second) * grads * grads
    first_hat = new_momentum / (1.0 - jnp.power(jnp.float32(beta_first), counted))
    second_hat = new_variance / (1.0 - jnp.power(jnp.float32(beta_second), counted))
    update = learn_rate * (first_hat / (jnp.sqrt(second_hat) + adam_eps) + decay_rate * params)
    return (params - update, new_momentum, new_variance)


OFFSETS = [(0, 0), (0, 1), (-1, 0), (1, 0), (-1, 1), (1, 1), (2, 0), (2, 1)]


def tied(*values):
    return lax.optimization_barrier(values)


def turn_kernel(rows, slots_ref, up_ref, mine_ref, theirs_ref):
    core = slots_ref[0]
    for chip in range(NY * NX):
        for side in range(NC):
            first = (chip * NC + side) * rows
            left = first // 128 * 128
            right = -(-(first + rows) // 128) * 128
            turned = up_ref[:, left:right].T[first - left : first - left + rows]

            @pl.when(core == side)
            def _():
                mine_ref[slots_ref[1 + chip]] = turned

            @pl.when(core != side)
            def _():
                theirs_ref[slots_ref[1 + chip]] = turned


def turned_blocks(upstream, rows, slots):
    tokens, width = upstream.shape
    shape = jax.ShapeDtypeStruct((NY * NX, rows, tokens), upstream.dtype)
    return pl.pallas_call(
        partial(turn_kernel, rows),
        out_shape=(shape, shape),
        in_specs=[
            pl.BlockSpec(memory_space=pltpu.SMEM),
            pl.BlockSpec(memory_space=pltpu.VMEM),
        ],
        out_specs=(
            pl.BlockSpec(memory_space=pltpu.VMEM),
            pl.BlockSpec(memory_space=pltpu.VMEM),
        ),
        compiler_params=pltpu.CompilerParams(
            vmem_limit_bytes=vmem_limit(upstream, shape, shape)
        ),
        cost_estimate=NO_COST,
    )(slots, upstream)


def vmem_limit(*arrays):
    total = 0
    for array in arrays:
        *outer, above, last = (1,) + tuple(array.shape)
        held = -(-above // 16) * 16 * -(-last // 128) * 128
        for size in outer:
            held *= size
        total += held * jnp.dtype(array.dtype).itemsize
    return total + (4 << 20)


def local_call(kernel, out_shape, scratch=(), cost=NO_COST):
    whole = pl.BlockSpec(memory_space=pltpu.VMEM)

    def call(*operands):
        return pl.pallas_call(
            kernel,
            out_shape=out_shape,
            in_specs=[whole] * len(operands),
            out_specs=jax.tree.map(lambda _: whole, out_shape),
            scratch_shapes=[pltpu.VMEM(held.shape, held.dtype) for held in scratch],
            compiler_params=pltpu.CompilerParams(
                vmem_limit_bytes=vmem_limit(*out_shape, *scratch) + EXTRA_BYTES
            ),
            cost_estimate=cost,
        )(*operands)

    return call


def join_kernel(own_ref, other_ref, joined_ref, turned_ref):
    tokens, features = own_ref.shape
    for part, ref in enumerate((own_ref, other_ref)):
        at = slice(part * tokens, (part + 1) * tokens)
        joined_ref[at] = ref[...]
        for first in range(0, features, 256):
            turned_ref[first : first + 256, at] = ref[:, first : first + 256].T


def joined_tokens(own, other):
    tokens, features = own.shape
    return local_call(
        join_kernel,
        (
            jax.ShapeDtypeStruct((NC * tokens, features), own.dtype),
            jax.ShapeDtypeStruct((features, NC * tokens), own.dtype),
        ),
    )(own, other)


def gain_column(block_ref, rows):
    wide = -(-rows // 128) * 128
    return block_ref[rows : rows + GAIN_ROWS, :wide].astype(jnp.float32).T[:rows, :1]


def forward_kernel(k, rows, block_ref, attn_ref, mine_ref, given_ref, out_ref, stat_ref):
    tokens = mine_ref.shape[2]
    gain = gain_column(block_ref, rows)
    for part, up_ref in enumerate((mine_ref, given_ref)):
        at = slice(part * tokens, (part + 1) * tokens)
        out = jnp.dot(block_ref[:rows], attn_ref[:, at], preferred_element_type=jnp.float32)
        out_ref[:, at] = out
        scaled = up_ref[k].astype(jnp.float32) * gain
        stat_ref[0:1, at] = jnp.sum(out * out, 0, keepdims=True)
        stat_ref[1:2, at] = jnp.sum(out * scaled, 0, keepdims=True)


def forward_block(k, rows, block, attn, mine, given, cost):
    count = attn.shape[1]
    return local_call(
        partial(forward_kernel, k, rows),
        (
            jax.ShapeDtypeStruct((rows, count), jnp.float32),
            jax.ShapeDtypeStruct((2, count), jnp.float32),
        ),
        cost=cost,
    )(block, attn, mine, given)


def weight_kernel(k, rows, width, *refs):
    sums_ref, other_sums_ref, mine_ref, given_ref, attn_ref, out_ref, block_ref = refs[:7]
    grad_ref, gain_ref = refs[7:9]
    term_refs = refs[9:]
    tokens = mine_ref.shape[2]
    gain = gain_column(block_ref, rows)
    folded = jnp.zeros((rows, 128), jnp.float32)
    for part, up_ref in enumerate((mine_ref, given_ref)):
        here = slice(part * tokens, (part + 1) * tokens)
        there = slice((1 - part) * tokens, (2 - part) * tokens)
        inverse_row = lax.rsqrt(
            (sums_ref[0:1, here] + other_sums_ref[0:1, there]) / width + norm_eps
        )
        slope_row = (sums_ref[1:2, here] + other_sums_ref[1:2, there]) / width
        slope_row = slope_row * inverse_row * inverse_row
        for first in range(0, tokens, 128):
            inverse = inverse_row[:, first : first + 128]
            slope = slope_row[:, first : first + 128]
            at = slice(part * tokens + first, part * tokens + first + 128)
            out = out_ref[:, at]
            up = up_ref[k, :, first : first + 128].astype(jnp.float32)
            grad = inverse * (up * gain - out * slope)
            grad_ref[:, at] = grad.astype(grad_ref.dtype)
            folded = folded + up * (out * inverse)
    gain_ref[...] = jnp.sum(folded.T, 0, keepdims=True)
    begin = 0
    for term_ref in term_refs:
        for first in range(0, term_ref.shape[1], 256):
            columns = slice(begin + first, begin + first + 256)
            term_ref[:, first : first + 256] = jnp.dot(
                grad_ref[...], attn_ref[:, columns], preferred_element_type=jnp.float32
            ).astype(term_ref.dtype)
        begin += term_ref.shape[1]


def weight_block(k, rows, width, cuts, sums, other_sums, mine, given, attn, out, block):
    tokens, features = attn.shape
    edges = (0,) + cuts + (features,)
    got = local_call(
        partial(weight_kernel, k, rows, width),
        (
            jax.ShapeDtypeStruct((rows, tokens), mine.dtype),
            jax.ShapeDtypeStruct((1, rows), jnp.float32),
        )
        + tuple(
            jax.ShapeDtypeStruct((rows, end - begin), mine.dtype)
            for begin, end in zip(edges, edges[1:])
        ),
    )(sums, other_sums, mine, given, attn, out, block)
    return got[0], got[1][0], got[2:]


def input_kernel(rows, tokens, count, *refs):
    grad_refs, block_refs = refs[:count], refs[count : 2 * count]
    own_ref, theirs_ref, turned, held = refs[2 * count :]
    features = own_ref.shape[1]
    step = held.shape[1]
    for first in range(0, count * rows, 256):
        parts = []
        for j in range(count):
            low, high = max(first, j * rows), min(first + 256, (j + 1) * rows)
            if low < high:
                parts.append(grad_refs[j][low - j * rows : high - j * rows])
        turned[:, first : first + 256] = jnp.concatenate(parts).T
    for first in range(0, features, step):
        for j in range(count):
            held[j * rows : (j + 1) * rows] = block_refs[j][:rows, first : first + step]
        for part, out_ref in enumerate((own_ref, theirs_ref)):
            out_ref[:, first : first + step] = jnp.dot(
                turned[part * tokens : (part + 1) * tokens],
                held[...],
                preferred_element_type=jnp.float32,
            ).astype(out_ref.dtype)


def input_grads(rows, tokens, grads, blocks):
    features = blocks[0].shape[1]
    low = blocks[0].dtype
    count = len(blocks)
    return local_call(
        partial(input_kernel, rows, tokens, count),
        (
            jax.ShapeDtypeStruct((tokens, features), low),
            jax.ShapeDtypeStruct((tokens, features), low),
        ),
        (
            jax.ShapeDtypeStruct((NC * tokens, count * rows), low),
            jax.ShapeDtypeStruct((count * rows, 512), low),
        ),
    )(*grads, *blocks)


def plus(first, *others):
    total = first.astype(jnp.float32)
    for one in others:
        total = total + one.astype(jnp.float32)
    return total


def shards(
    attention,
    upstream,
    step_index,
    weight,
    weight_momentum,
    weight_variance,
    norm_gain,
    gain_momentum,
    gain_variance,
):
    rows, features = weight.shape[1:]
    tokens, width = upstream.shape[1:]
    half = rows // 2
    low = jnp.bfloat16
    index = lax.axis_index("fsdp")
    core = index % NC
    x = index // NC % NX
    y = index // (NC * NX)

    gain_rows = jnp.pad(norm_gain.astype(low), ((0, GAIN_ROWS - 1), (0, features - rows)))
    (own,) = tied(jnp.concatenate([weight[0].astype(low), gain_rows]))
    below = move(own, dy=1)
    above = move(own, dy=-1)
    across = move(own, dx=1)
    attn_other = move(attention[0], dcore=1)

    chips = jnp.arange(NY * NX)
    away = (chips // NX - y) % NY * NX + (chips % NX - x) % NX
    order = [0] * (NY * NX)
    for k, (dy, dx) in enumerate(OFFSETS):
        order[dy % NY * NX + dx] = k
    slots = jnp.concatenate(
        [core[None], jnp.array(order, jnp.int32)[away]]
    ).astype(jnp.int32)
    mine, theirs = turned_blocks(upstream[0], rows, slots)
    attn, attn_turned = joined_tokens(attention[0], attn_other)

    below, above, across, mine, theirs, attn_turned = tied(
        below, above, across, mine, theirs, attn_turned
    )
    far_top = move(below[:half], dy=1)
    far_bottom = move(above[half:], dy=-1)
    given = move(theirs, dcore=1)
    outs = [None] * 8
    sums = [None] * 8

    def run(k, block, cost=NO_COST):
        outs[k], sums[k] = forward_block(k, rows, block, attn_turned, mine, given, cost)

    run(0, own)
    across, outs[0] = tied(across, outs[0])
    across_below = move(across, dy=1)
    across_above = move(across, dy=-1)
    far = jnp.concatenate([far_top, far_bottom])
    across_far = move(far, dx=1)
    for k, block in [(1, across), (2, below), (3, above), (6, far)]:
        run(k, block)
    across_below, across_above, *outs[1:4], outs[6] = tied(
        across_below, across_above, *outs[1:4], outs[6]
    )
    for k, block in [(4, across_below), (5, across_above)]:
        run(k, block, SMALL_COST)
    across_far, *outs[4:6] = tied(across_far, *outs[4:6])
    run(7, across_far)
    blocks = [own, across, below, above, across_below, across_above, far, across_far]
    sums = sum(sums[1:], sums[0])
    other_sums = move(sums, dcore=1)

    left, right = slice(0, CUT), slice(CUT, features)
    grads = [None] * 8
    gain_parts = [None] * 8

    def run_weight(k, *cuts):
        grads[k], gain_parts[k], terms = weight_block(
            k, rows, width, cuts, sums, other_sums, mine, given, attn, outs[k], blocks[k]
        )
        return terms

    own_across_far = run_weight(7)
    own_across_below = run_weight(4)
    own_across_above = run_weight(5)
    across_far = move(own_across_far[0], dx=1)
    from_above = move(own_across_below[0], dy=-1)
    from_below = move(own_across_above[0], dy=1)
    sums, grads[7], grads[4], grads[5] = tied(sums, grads[7], grads[4], grads[5])
    middle = features // 2
    far_left, far_right = run_weight(6, middle)
    (own_across,) = run_weight(1)
    below_left, below_middle, below_right = run_weight(2, CUT, middle)
    above_left, above_middle, above_right = run_weight(3, CUT, middle)
    own_left, own_right = run_weight(0, CUT)
    gain_own, gain_across, gain_below, gain_above, *gain_rest = gain_parts
    gain_moved = move(jnp.stack([gain_rest[2], gain_rest[3], gain_below, gain_rest[0]]), dy=2)
    input_own, input_theirs = input_grads(rows, tokens, grads, blocks)
    across_far, from_above, from_below, gain_moved, input_own, input_theirs = tied(
        across_far, from_above, from_below, gain_moved, input_own, input_theirs
    )

    far_down = move(plus(far_left, across_far[:, :middle]).astype(low), dy=-1)
    far_up = move(plus(far_right, across_far[:, middle:]).astype(low), dy=1)
    side = move(plus(own_across, from_above, from_below).astype(low), dx=1)
    gain_up = jnp.stack([gain_above, gain_rest[1]]) + gain_moved[2:]
    gain_up = move(gain_up, dy=1)
    input_given = move(input_theirs, dcore=1)
    far_down, far_up, gain_up, input_given, above_left, below_right = tied(
        far_down, far_up, gain_up, input_given, above_left, below_right
    )
    downs = [
        plus(below_left, far_down[:, :CUT]).astype(low),
        jnp.concatenate([plus(below_middle, far_down[:, CUT:]).astype(low), below_right], 1),
    ]
    ups = [
        above_left,
        jnp.concatenate([above_middle, plus(above_right, far_up).astype(low)], 1),
    ]
    downs = [move(part, dy=-1) for part in downs]
    ups = [move(part, dy=1) for part in ups]
    grad_input = plus(input_own, input_given).astype(low)
    gain_pair = jnp.stack([gain_own, gain_across]) + gain_moved[:2] + gain_up
    side, downs[0], ups[0], gain_pair, grad_input = tied(
        side, downs[0], ups[0], gain_pair, grad_input
    )
    gain_side = move(gain_pair[1], dx=1)
    results = []
    peers = []
    for columns, own_term, down, up in zip((left, right), (own_left, own_right), downs, ups):
        if results:
            down, up, gain_side, peers = tied(down, up, gain_side, peers)
            local_gain, new_gain_momentum, new_gain_variance = adam_update(
                norm_gain,
                (gain_pair[0] + gain_side)[None],
                gain_momentum,
                gain_variance,
                step_index,
            )
        results.append(
            adam_update(
                weight[0, :, columns],
                plus(own_term, side[:, columns], down, up),
                weight_momentum[0, :, columns],
                weight_variance[0, :, columns],
                step_index,
            )
        )
        sent = (results[-1][0].astype(low),)
        if peers:
            sent += (local_gain,)
        peers += swapped(sent, step_index)
    locals_, momenta, variances = zip(*results)
    new_weight = jnp.concatenate([0.5 * plus(a, b) for a, b in zip(locals_, peers)], 1)[None]
    new_weight_momentum = jnp.concatenate(momenta, 1)[None]
    new_weight_variance = jnp.concatenate(variances, 1)[None]
    new_gain = 0.5 * (local_gain + peers[2])
    return (
        grad_input[None],
        new_weight,
        new_weight_momentum,
        new_weight_variance,
        new_gain,
        new_gain_momentum,
        new_gain_variance,
    )


def solution(mesh):
    block = P("replica", "fsdp", None)
    vector = P("replica", "fsdp")
    return jax.shard_map(
        shards,
        mesh=mesh,
        in_specs=(block, block, P(), block, block, block, vector, vector, vector),
        out_specs=(block, block, block, block, vector, vector, vector),
        check_vma=False,
    )
```

```python
from functools import partial

import jax
import jax.numpy as jnp
from jax import lax
from jax.experimental import pallas as pl
from jax.experimental.pallas import tpu as pltpu
from jax.sharding import PartitionSpec as P

learn_rate = 0.001
beta_first = 0.9
beta_second = 0.999
decay_rate = 0.1
adam_eps = 1e-08
norm_eps = 1e-06

NY, NX, NC = 4, 2, 2
CUT = 768
GAIN_ROWS = 8
EXTRA_BYTES = 0
NO_COST = pl.CostEstimate(flops=0, bytes_accessed=0, transcendentals=0)
SMALL_COST = pl.CostEstimate(flops=1_200_000_000, bytes_accessed=0, transcendentals=0)


def place(y, x, core):
    return ((y % NY) * NX + x % NX) * NC + core % NC


def route(dy, dx, dcore):
    return [
        (place(y, x, core), place(y + dy, x + dx, core + dcore))
        for y in range(NY)
        for x in range(NX)
        for core in range(NC)
    ]


def move(block, dy=0, dx=0, dcore=0):
    return lax.ppermute(block, "fsdp", route(dy, dx, dcore))


def swapped(values, step_index):
    count = lax.axis_size("replica")
    levels = count.bit_length() - 1

    def swap(level, *parts):
        pairs = [(low, low ^ (1 << level)) for low in range(count)]
        return tuple(lax.ppermute(part, "replica", pairs) for part in parts)

    return lax.switch(
        step_index % levels, [partial(swap, level) for level in range(levels)], *values
    )


def adam_update(params, grads, momentum, variance, step_index):
    counted = (step_index + 1).astype(jnp.float32)
    new_momentum = beta_first * momentum + (1.0 - beta_first) * grads
    new_variance = beta_second * variance + (1.0 - beta_second) * grads * grads
    first_hat = new_momentum / (1.0 - jnp.power(jnp.float32(beta_first), counted))
    second_hat = new_variance / (1.0 - jnp.power(jnp.float32(beta_second), counted))
    update = learn_rate * (first_hat / (jnp.sqrt(second_hat) + adam_eps) + decay_rate * params)
    return (params - update, new_momentum, new_variance)


OFFSETS = [(0, 0), (0, 1), (-1, 0), (1, 0), (-1, 1), (1, 1), (2, 0), (2, 1)]


def tied(*values):
    return lax.optimization_barrier(values)


def turn_kernel(rows, slots_ref, up_ref, mine_ref, theirs_ref):
    core = slots_ref[0]
    for chip in range(NY * NX):
        for side in range(NC):
            first = (chip * NC + side) * rows
            left = first // 128 * 128
            right = -(-(first + rows) // 128) * 128
            turned = up_ref[:, left:right].T[first - left : first - left + rows]

            @pl.when(core == side)
            def _():
                mine_ref[slots_ref[1 + chip]] = turned

            @pl.when(core != side)
            def _():
                theirs_ref[slots_ref[1 + chip]] = turned


def turned_blocks(upstream, rows, slots):
    tokens, width = upstream.shape
    shape = jax.ShapeDtypeStruct((NY * NX, rows, tokens), upstream.dtype)
    return pl.pallas_call(
        partial(turn_kernel, rows),
        out_shape=(shape, shape),
        in_specs=[
            pl.BlockSpec(memory_space=pltpu.SMEM),
            pl.BlockSpec(memory_space=pltpu.VMEM),
        ],
        out_specs=(
            pl.BlockSpec(memory_space=pltpu.VMEM),
            pl.BlockSpec(memory_space=pltpu.VMEM),
        ),
        compiler_params=pltpu.CompilerParams(
            vmem_limit_bytes=vmem_limit(upstream, shape, shape)
        ),
        cost_estimate=NO_COST,
    )(slots, upstream)


def vmem_limit(*arrays):
    total = 0
    for array in arrays:
        *outer, above, last = (1,) + tuple(array.shape)
        held = -(-above // 16) * 16 * -(-last // 128) * 128
        for size in outer:
            held *= size
        total += held * jnp.dtype(array.dtype).itemsize
    return total + (4 << 20)


def local_call(kernel, out_shape, scratch=(), cost=NO_COST):
    whole = pl.BlockSpec(memory_space=pltpu.VMEM)

    def call(*operands):
        return pl.pallas_call(
            kernel,
            out_shape=out_shape,
            in_specs=[whole] * len(operands),
            out_specs=jax.tree.map(lambda _: whole, out_shape),
            scratch_shapes=[pltpu.VMEM(held.shape, held.dtype) for held in scratch],
            compiler_params=pltpu.CompilerParams(
                vmem_limit_bytes=vmem_limit(*out_shape, *scratch) + EXTRA_BYTES
            ),
            cost_estimate=cost,
        )(*operands)

    return call


def stack_kernel(count, *refs):
    for pair, out_ref in zip(zip(refs[: 2 * count : 2], refs[1 : 2 * count : 2]), refs[2 * count :]):
        first = 0
        for ref in pair:
            out_ref[first : first + ref.shape[0]] = ref[...]
            first += ref.shape[0]


def stacked_halves(*pairs):
    shape = [
        jax.ShapeDtypeStruct((top.shape[0] + bottom.shape[0], top.shape[1]), top.dtype)
        for top, bottom in pairs
    ]
    flat = [half for pair in pairs for half in pair]
    return local_call(partial(stack_kernel, len(pairs)), tuple(shape), cost=SMALL_COST)(*flat)


def pack_kernel(weight_ref, gain_ref, top_ref, bottom_ref, whole_ref):
    half = top_ref.shape[0]
    rows, features = weight_ref.shape
    low = whole_ref.dtype
    top = weight_ref[:half].astype(low)
    bottom = weight_ref[half:].astype(low)
    gain = jnp.broadcast_to(gain_ref[...], (GAIN_ROWS, features)).astype(low)
    top_ref[...] = top
    bottom_ref[: rows - half] = bottom
    bottom_ref[rows - half :] = gain
    whole_ref[:half] = top
    whole_ref[half:rows] = bottom
    whole_ref[rows:] = gain


def packed_rows(weight, gain_row):
    rows, features = weight.shape
    half = rows // 2
    return local_call(
        pack_kernel,
        tuple(
            jax.ShapeDtypeStruct((count, features), jnp.bfloat16)
            for count in (half, rows - half + GAIN_ROWS, rows + GAIN_ROWS)
        ),
    )(weight, gain_row)


def join_kernel(own_ref, other_ref, joined_ref, turned_ref):
    tokens, features = own_ref.shape
    for part, ref in enumerate((own_ref, other_ref)):
        at = slice(part * tokens, (part + 1) * tokens)
        joined_ref[at] = ref[...]
        for first in range(0, features, 256):
            turned_ref[first : first + 256, at] = ref[:, first : first + 256].T


def joined_tokens(own, other):
    tokens, features = own.shape
    return local_call(
        join_kernel,
        (
            jax.ShapeDtypeStruct((NC * tokens, features), own.dtype),
            jax.ShapeDtypeStruct((features, NC * tokens), own.dtype),
        ),
    )(own, other)


def gain_column(block_ref, rows):
    wide = -(-rows // 128) * 128
    return block_ref[rows : rows + GAIN_ROWS, :wide].astype(jnp.float32).T[:rows, :1]


def forward_kernel(k, rows, block_ref, attn_ref, mine_ref, given_ref, out_ref, stat_ref):
    tokens = mine_ref.shape[2]
    gain = gain_column(block_ref, rows)
    for part, up_ref in enumerate((mine_ref, given_ref)):
        at = slice(part * tokens, (part + 1) * tokens)
        out = jnp.dot(block_ref[:rows], attn_ref[:, at], preferred_element_type=jnp.float32)
        out_ref[:, at] = out
        scaled = up_ref[k].astype(jnp.float32) * gain
        stat_ref[0:1, at] = jnp.sum(out * out, 0, keepdims=True)
        stat_ref[1:2, at] = jnp.sum(out * scaled, 0, keepdims=True)


def forward_block(k, rows, block, attn, mine, given, cost):
    count = attn.shape[1]
    return local_call(
        partial(forward_kernel, k, rows),
        (
            jax.ShapeDtypeStruct((rows, count), jnp.float32),
            jax.ShapeDtypeStruct((2, count), jnp.float32),
        ),
        cost=cost,
    )(block, attn, mine, given)


def weight_kernel(k, rows, width, *refs):
    sums_ref, other_sums_ref, mine_ref, given_ref, attn_ref, out_ref, block_ref = refs[:7]
    grad_ref, gain_ref = refs[7:9]
    term_refs = refs[9:]
    tokens = mine_ref.shape[2]
    gain = gain_column(block_ref, rows)
    folded = jnp.zeros((rows, 128), jnp.float32)
    for part, up_ref in enumerate((mine_ref, given_ref)):
        here = slice(part * tokens, (part + 1) * tokens)
        there = slice((1 - part) * tokens, (2 - part) * tokens)
        inverse_row = lax.rsqrt(
            (sums_ref[0:1, here] + other_sums_ref[0:1, there]) / width + norm_eps
        )
        slope_row = (sums_ref[1:2, here] + other_sums_ref[1:2, there]) / width
        slope_row = slope_row * inverse_row * inverse_row
        for first in range(0, tokens, 128):
            inverse = inverse_row[:, first : first + 128]
            slope = slope_row[:, first : first + 128]
            at = slice(part * tokens + first, part * tokens + first + 128)
            out = out_ref[:, at]
            up = up_ref[k, :, first : first + 128].astype(jnp.float32)
            grad = inverse * (up * gain - out * slope)
            grad_ref[:, at] = grad.astype(grad_ref.dtype)
            folded = folded + up * (out * inverse)
    gain_ref[...] = jnp.sum(folded.T, 0, keepdims=True)
    begin = 0
    for term_ref in term_refs:
        for first in range(0, term_ref.shape[1], 256):
            columns = slice(begin + first, begin + first + 256)
            term_ref[:, first : first + 256] = jnp.dot(
                grad_ref[...], attn_ref[:, columns], preferred_element_type=jnp.float32
            ).astype(term_ref.dtype)
        begin += term_ref.shape[1]


def weight_block(k, rows, width, cuts, sums, other_sums, mine, given, attn, out, block):
    tokens, features = attn.shape
    edges = (0,) + cuts + (features,)
    got = local_call(
        partial(weight_kernel, k, rows, width),
        (
            jax.ShapeDtypeStruct((rows, tokens), mine.dtype),
            jax.ShapeDtypeStruct((1, rows), jnp.float32),
        )
        + tuple(
            jax.ShapeDtypeStruct((rows, end - begin), mine.dtype)
            for begin, end in zip(edges, edges[1:])
        ),
    )(sums, other_sums, mine, given, attn, out, block)
    return got[0], got[1][0], got[2:]


def input_kernel(part, rows, count, *refs):
    grad_refs, block_refs = refs[:count], refs[count : 2 * count]
    given_refs = refs[2 * count : -3]
    out_ref, turned, held = refs[-3:]
    tokens, features = out_ref.shape
    step = held.shape[1]
    at = slice(part * tokens, (part + 1) * tokens)
    for first in range(0, count * rows, 256):
        parts = []
        for j in range(count):
            low, high = max(first, j * rows), min(first + 256, (j + 1) * rows)
            if low < high:
                parts.append(grad_refs[j][low - j * rows : high - j * rows, at])
        turned[:, first : first + 256] = jnp.concatenate(parts).T
    for first in range(0, features, step):
        columns = slice(first, first + step)
        for j in range(count):
            held[j * rows : (j + 1) * rows] = block_refs[j][:rows, columns]
        total = jnp.dot(turned[...], held[...], preferred_element_type=jnp.float32)
        for given_ref in given_refs:
            total = total + given_ref[:, columns].astype(jnp.float32)
        out_ref[:, columns] = total.astype(out_ref.dtype)


def input_grads(part, rows, tokens, grads, blocks, given=()):
    features = blocks[0].shape[1]
    low = blocks[0].dtype
    count = len(blocks)
    return local_call(
        partial(input_kernel, part, rows, count),
        (jax.ShapeDtypeStruct((tokens, features), low),),
        (
            jax.ShapeDtypeStruct((tokens, count * rows), low),
            jax.ShapeDtypeStruct((count * rows, 512), low),
        ),
    )(*grads, *blocks, *given)[0]


def plus(first, *others):
    total = first.astype(jnp.float32)
    for one in others:
        total = total + one.astype(jnp.float32)
    return total


def shards(
    attention,
    upstream,
    step_index,
    weight,
    weight_momentum,
    weight_variance,
    norm_gain,
    gain_momentum,
    gain_variance,
):
    rows, features = weight.shape[1:]
    tokens, width = upstream.shape[1:]
    half = rows // 2
    low = jnp.bfloat16
    index = lax.axis_index("fsdp")
    core = index % NC
    x = index // NC % NX
    y = index // (NC * NX)

    gain_row = jnp.pad(norm_gain, ((0, 0), (0, features - rows)))
    own_top, own_bottom, own = packed_rows(weight[0], gain_row)
    below_top = move(own_top, dy=1)
    above_bottom = move(own_bottom, dy=-1)
    below_bottom = move(own_bottom, dy=1)
    above_top = move(own_top, dy=-1)
    across = move(own, dx=1)

    chips = jnp.arange(NY * NX)
    away = (chips // NX - y) % NY * NX + (chips % NX - x) % NX
    order = [0] * (NY * NX)
    for k, (dy, dx) in enumerate(OFFSETS):
        order[dy % NY * NX + dx] = k
    slots = jnp.concatenate(
        [core[None], jnp.array(order, jnp.int32)[away]]
    ).astype(jnp.int32)
    mine, theirs = turned_blocks(upstream[0], rows, slots)

    below_top, above_bottom, mine, theirs = tied(below_top, above_bottom, mine, theirs)
    far_top = move(below_top, dy=1)
    far_bottom = move(above_bottom, dy=-1)
    below, above = stacked_halves((below_top, below_bottom), (above_top, above_bottom))

    far_top, far_bottom, below, above, across = tied(far_top, far_bottom, below, above, across)
    far = jnp.concatenate([far_top, far_bottom])
    across_below = move(across, dy=1)
    across_above = move(across, dy=-1)
    across_far = move(far, dx=1)
    attention_own, theirs, _ = tied(attention[0], theirs, across)
    attn_other = move(attention_own, dcore=1)
    given = move(theirs, dcore=1)
    attn, attn_turned = joined_tokens(attention_own, attn_other)
    outs = [None] * 8
    sums = [None] * 8

    def run(k, block, cost=NO_COST):
        outs[k], sums[k] = forward_block(k, rows, block, attn_turned, mine, given, cost)

    for k, block in [(0, own), (1, across), (2, below), (3, above), (6, far)]:
        run(k, block)
    across_below, across_above, *outs[:4], outs[6] = tied(
        across_below, across_above, *outs[:4], outs[6]
    )
    for k, block in [(4, across_below), (5, across_above)]:
        run(k, block, SMALL_COST)
    across_far, *outs[4:6] = tied(across_far, *outs[4:6])
    run(7, across_far)
    blocks = [own, across, below, above, across_below, across_above, far, across_far]
    sums = sum(sums[1:], sums[0])
    other_sums = move(sums, dcore=1)

    left, right = slice(0, CUT), slice(CUT, features)
    grads = [None] * 8
    gain_parts = [None] * 8

    def run_weight(k, *cuts):
        grads[k], gain_parts[k], terms = weight_block(
            k, rows, width, cuts, sums, other_sums, mine, given, attn, outs[k], blocks[k]
        )
        return terms

    own_across_far = run_weight(7)
    own_across_below = run_weight(4)
    own_across_above = run_weight(5)
    across_far = move(own_across_far[0], dx=1)
    from_above = move(own_across_below[0], dy=-1)
    from_below = move(own_across_above[0], dy=1)
    sums, grads[7], grads[4], grads[5] = tied(sums, grads[7], grads[4], grads[5])
    middle = features // 2
    far_left, far_right = run_weight(6, middle)
    (own_across,) = run_weight(1)
    below_left, below_middle, below_right = run_weight(2, CUT, middle)
    above_left, above_middle, above_right = run_weight(3, CUT, middle)
    own_left, own_right = run_weight(0, CUT)
    gain_own, gain_across, gain_below, gain_above, *gain_rest = gain_parts
    gain_moved = move(jnp.stack([gain_rest[2], gain_rest[3], gain_below, gain_rest[0]]), dy=2)
    input_theirs = input_grads(1, rows, tokens, grads, blocks)
    across_far, from_above, from_below, gain_moved, input_theirs = tied(
        across_far, from_above, from_below, gain_moved, input_theirs
    )

    far_down = move(plus(far_left, across_far[:, :middle]).astype(low), dy=-1)
    far_up = move(plus(far_right, across_far[:, middle:]).astype(low), dy=1)
    side = move(plus(own_across, from_above, from_below).astype(low), dx=1)
    gain_up = jnp.stack([gain_above, gain_rest[1]]) + gain_moved[2:]
    gain_up = move(gain_up, dy=1)
    input_given = move(input_theirs, dcore=1)
    grad_input = input_grads(0, rows, tokens, grads, blocks, (input_given,))
    far_down, far_up, gain_up, grad_input, above_left, below_right = tied(
        far_down, far_up, gain_up, grad_input, above_left, below_right
    )
    downs = [
        plus(below_left, far_down[:, :CUT]).astype(low),
        jnp.concatenate([plus(below_middle, far_down[:, CUT:]).astype(low), below_right], 1),
    ]
    ups = [
        above_left,
        jnp.concatenate([above_middle, plus(above_right, far_up).astype(low)], 1),
    ]
    downs = [move(part, dy=-1) for part in downs]
    ups = [move(part, dy=1) for part in ups]
    gain_pair = jnp.stack([gain_own, gain_across]) + gain_moved[:2] + gain_up
    side, downs[0], ups[0], gain_pair = tied(side, downs[0], ups[0], gain_pair)
    gain_side = move(gain_pair[1], dx=1)
    grad_left = plus(own_left, side[:, left], downs[0], ups[0])
    local_left = adam_update(
        weight[0, :, left],
        grad_left,
        weight_momentum[0, :, left],
        weight_variance[0, :, left],
        step_index,
    )[0]
    (peer_left,) = swapped((local_left.astype(low),), step_index)
    downs, ups, gain_side, peer_left = tied(downs, ups, gain_side, peer_left)
    local_gain, new_gain_momentum, new_gain_variance = adam_update(
        norm_gain, (gain_pair[0] + gain_side)[None], gain_momentum, gain_variance, step_index
    )
    grad_weight = jnp.concatenate(
        [
            plus(own_left, side[:, left], downs[0], ups[0]),
            plus(own_right, side[:, right], downs[1], ups[1]),
        ],
        1,
    )[None]
    local_weight, new_weight_momentum, new_weight_variance = adam_update(
        weight, grad_weight, weight_momentum, weight_variance, step_index
    )
    peer_right, peer_gain = swapped((local_weight[0, :, right].astype(low), local_gain), step_index)
    peer_weight = jnp.concatenate([peer_left, peer_right], 1)[None]
    new_weight = 0.5 * plus(local_weight, peer_weight)
    new_gain = 0.5 * (local_gain + peer_gain)
    return (
        grad_input[None],
        new_weight,
        new_weight_momentum,
        new_weight_variance,
        new_gain,
        new_gain_momentum,
        new_gain_variance,
    )


def solution(mesh):
    block = P("replica", "fsdp", None)
    vector = P("replica", "fsdp")
    return jax.shard_map(
        shards,
        mesh=mesh,
        in_specs=(block, block, P(), block, block, block, vector, vector, vector),
        out_specs=(block, block, block, block, vector, vector, vector),
        check_vma=False,
    )
```

```python
from functools import partial

import jax
import jax.numpy as jnp
from jax import lax
from jax.experimental import pallas as pl
from jax.experimental.pallas import tpu as pltpu
from jax.sharding import PartitionSpec as P

learn_rate = 0.001
beta_first = 0.9
beta_second = 0.999
decay_rate = 0.1
adam_eps = 1e-08
norm_eps = 1e-06

NY, NX, NC = 4, 2, 2
CUT = 768
GAIN_ROWS = 8
EXTRA_BYTES = 0
NO_COST = pl.CostEstimate(flops=0, bytes_accessed=0, transcendentals=0)
SMALL_COST = pl.CostEstimate(flops=1_200_000_000, bytes_accessed=0, transcendentals=0)


def place(y, x, core):
    return ((y % NY) * NX + x % NX) * NC + core % NC


def route(dy, dx, dcore):
    return [
        (place(y, x, core), place(y + dy, x + dx, core + dcore))
        for y in range(NY)
        for x in range(NX)
        for core in range(NC)
    ]


def move(block, dy=0, dx=0, dcore=0):
    return lax.ppermute(block, "fsdp", route(dy, dx, dcore))


def swapped(values, step_index):
    count = lax.axis_size("replica")
    levels = count.bit_length() - 1

    def swap(level, *parts):
        pairs = [(low, low ^ (1 << level)) for low in range(count)]
        return tuple(lax.ppermute(part, "replica", pairs) for part in parts)

    return lax.switch(
        step_index % levels, [partial(swap, level) for level in range(levels)], *values
    )


def adam_update(params, grads, momentum, variance, step_index):
    counted = (step_index + 1).astype(jnp.float32)
    new_momentum = beta_first * momentum + (1.0 - beta_first) * grads
    new_variance = beta_second * variance + (1.0 - beta_second) * grads * grads
    first_hat = new_momentum / (1.0 - jnp.power(jnp.float32(beta_first), counted))
    second_hat = new_variance / (1.0 - jnp.power(jnp.float32(beta_second), counted))
    update = learn_rate * (first_hat / (jnp.sqrt(second_hat) + adam_eps) + decay_rate * params)
    return (params - update, new_momentum, new_variance)


OFFSETS = [(0, 0), (0, 1), (-1, 0), (1, 0), (-1, 1), (1, 1), (2, 0), (2, 1)]


def tied(*values):
    return lax.optimization_barrier(values)


def turn_kernel(rows, slots_ref, up_ref, mine_ref, theirs_ref):
    core = slots_ref[0]
    for chip in range(NY * NX):
        for side in range(NC):
            first = (chip * NC + side) * rows
            left = first // 128 * 128
            right = -(-(first + rows) // 128) * 128
            turned = up_ref[:, left:right].T[first - left : first - left + rows]

            @pl.when(core == side)
            def _():
                mine_ref[slots_ref[1 + chip]] = turned

            @pl.when(core != side)
            def _():
                theirs_ref[slots_ref[1 + chip]] = turned


def turned_blocks(upstream, rows, slots):
    tokens, width = upstream.shape
    shape = jax.ShapeDtypeStruct((NY * NX, rows, tokens), upstream.dtype)
    return pl.pallas_call(
        partial(turn_kernel, rows),
        out_shape=(shape, shape),
        in_specs=[
            pl.BlockSpec(memory_space=pltpu.SMEM),
            pl.BlockSpec(memory_space=pltpu.VMEM),
        ],
        out_specs=(
            pl.BlockSpec(memory_space=pltpu.VMEM),
            pl.BlockSpec(memory_space=pltpu.VMEM),
        ),
        compiler_params=pltpu.CompilerParams(
            vmem_limit_bytes=vmem_limit(upstream, shape, shape)
        ),
        cost_estimate=NO_COST,
    )(slots, upstream)


def vmem_limit(*arrays):
    total = 0
    for array in arrays:
        *outer, above, last = (1,) + tuple(array.shape)
        held = -(-above // 16) * 16 * -(-last // 128) * 128
        for size in outer:
            held *= size
        total += held * jnp.dtype(array.dtype).itemsize
    return total + (4 << 20)


def local_call(kernel, out_shape, scratch=(), cost=NO_COST):
    whole = pl.BlockSpec(memory_space=pltpu.VMEM)

    def call(*operands):
        return pl.pallas_call(
            kernel,
            out_shape=out_shape,
            in_specs=[whole] * len(operands),
            out_specs=jax.tree.map(lambda _: whole, out_shape),
            scratch_shapes=[pltpu.VMEM(held.shape, held.dtype) for held in scratch],
            compiler_params=pltpu.CompilerParams(
                vmem_limit_bytes=vmem_limit(*out_shape, *scratch) + EXTRA_BYTES
            ),
            cost_estimate=cost,
        )(*operands)

    return call


def stack_kernel(count, *refs):
    for pair, out_ref in zip(zip(refs[: 2 * count : 2], refs[1 : 2 * count : 2]), refs[2 * count :]):
        first = 0
        for ref in pair:
            out_ref[first : first + ref.shape[0]] = ref[...]
            first += ref.shape[0]


def stacked_halves(*pairs):
    shape = [
        jax.ShapeDtypeStruct((top.shape[0] + bottom.shape[0], top.shape[1]), top.dtype)
        for top, bottom in pairs
    ]
    flat = [half for pair in pairs for half in pair]
    return local_call(partial(stack_kernel, len(pairs)), tuple(shape), cost=SMALL_COST)(*flat)


def pack_kernel(weight_ref, gain_ref, top_ref, bottom_ref, whole_ref):
    half = top_ref.shape[0]
    rows, features = weight_ref.shape
    low = whole_ref.dtype
    top = weight_ref[:half].astype(low)
    bottom = weight_ref[half:].astype(low)
    gain = jnp.broadcast_to(gain_ref[...], (GAIN_ROWS, features)).astype(low)
    top_ref[...] = top
    bottom_ref[: rows - half] = bottom
    bottom_ref[rows - half :] = gain
    whole_ref[:half] = top
    whole_ref[half:rows] = bottom
    whole_ref[rows:] = gain


def packed_rows(weight, gain_row):
    rows, features = weight.shape
    half = rows // 2
    return local_call(
        pack_kernel,
        tuple(
            jax.ShapeDtypeStruct((count, features), jnp.bfloat16)
            for count in (half, rows - half + GAIN_ROWS, rows + GAIN_ROWS)
        ),
    )(weight, gain_row)


def join_kernel(own_ref, other_ref, joined_ref, turned_ref):
    tokens, features = own_ref.shape
    for part, ref in enumerate((own_ref, other_ref)):
        at = slice(part * tokens, (part + 1) * tokens)
        joined_ref[at] = ref[...]
        for first in range(0, features, 256):
            turned_ref[first : first + 256, at] = ref[:, first : first + 256].T


def joined_tokens(own, other):
    tokens, features = own.shape
    return local_call(
        join_kernel,
        (
            jax.ShapeDtypeStruct((NC * tokens, features), own.dtype),
            jax.ShapeDtypeStruct((features, NC * tokens), own.dtype),
        ),
    )(own, other)


def gain_column(block_ref, rows):
    wide = -(-rows // 128) * 128
    return block_ref[rows : rows + GAIN_ROWS, :wide].astype(jnp.float32).T[:rows, :1]


def forward_kernel(k, rows, block_ref, attn_ref, mine_ref, given_ref, out_ref, stat_ref):
    tokens = mine_ref.shape[2]
    gain = gain_column(block_ref, rows)
    for part, up_ref in enumerate((mine_ref, given_ref)):
        at = slice(part * tokens, (part + 1) * tokens)
        out = jnp.dot(block_ref[:rows], attn_ref[:, at], preferred_element_type=jnp.float32)
        out_ref[:, at] = out
        scaled = up_ref[k].astype(jnp.float32) * gain
        stat_ref[0:1, at] = jnp.sum(out * out, 0, keepdims=True)
        stat_ref[1:2, at] = jnp.sum(out * scaled, 0, keepdims=True)


def forward_block(k, rows, block, attn, mine, given, cost):
    count = attn.shape[1]
    return local_call(
        partial(forward_kernel, k, rows),
        (
            jax.ShapeDtypeStruct((rows, count), jnp.float32),
            jax.ShapeDtypeStruct((2, count), jnp.float32),
        ),
        cost=cost,
    )(block, attn, mine, given)


def weight_kernel(k, rows, width, *refs):
    sums_ref, other_sums_ref, mine_ref, given_ref, attn_ref, out_ref, block_ref = refs[:7]
    grad_ref, gain_ref = refs[7:9]
    term_refs = refs[9:]
    tokens = mine_ref.shape[2]
    gain = gain_column(block_ref, rows)
    folded = jnp.zeros((rows, 128), jnp.float32)
    for part, up_ref in enumerate((mine_ref, given_ref)):
        here = slice(part * tokens, (part + 1) * tokens)
        there = slice((1 - part) * tokens, (2 - part) * tokens)
        inverse_row = lax.rsqrt(
            (sums_ref[0:1, here] + other_sums_ref[0:1, there]) / width + norm_eps
        )
        slope_row = (sums_ref[1:2, here] + other_sums_ref[1:2, there]) / width
        slope_row = slope_row * inverse_row * inverse_row
        for first in range(0, tokens, 128):
            inverse = inverse_row[:, first : first + 128]
            slope = slope_row[:, first : first + 128]
            at = slice(part * tokens + first, part * tokens + first + 128)
            out = out_ref[:, at]
            up = up_ref[k, :, first : first + 128].astype(jnp.float32)
            grad = inverse * (up * gain - out * slope)
            grad_ref[:, at] = grad.astype(grad_ref.dtype)
            folded = folded + up * (out * inverse)
    gain_ref[...] = jnp.sum(folded.T, 0, keepdims=True)
    begin = 0
    for term_ref in term_refs:
        for first in range(0, term_ref.shape[1], 256):
            columns = slice(begin + first, begin + first + 256)
            term_ref[:, first : first + 256] = jnp.dot(
                grad_ref[...], attn_ref[:, columns], preferred_element_type=jnp.float32
            ).astype(term_ref.dtype)
        begin += term_ref.shape[1]


def weight_block(k, rows, width, cuts, sums, other_sums, mine, given, attn, out, block):
    tokens, features = attn.shape
    edges = (0,) + cuts + (features,)
    got = local_call(
        partial(weight_kernel, k, rows, width),
        (
            jax.ShapeDtypeStruct((rows, tokens), mine.dtype),
            jax.ShapeDtypeStruct((1, rows), jnp.float32),
        )
        + tuple(
            jax.ShapeDtypeStruct((rows, end - begin), mine.dtype)
            for begin, end in zip(edges, edges[1:])
        ),
    )(sums, other_sums, mine, given, attn, out, block)
    return got[0], got[1][0], got[2:]


def input_kernel(rows, count, *refs):
    grad_refs, block_refs = refs[:count], refs[count : 2 * count]
    own_ref, theirs_ref, turned, held = refs[2 * count :]
    tokens, features = own_ref.shape
    step = held.shape[1]
    for first in range(0, count * rows, 256):
        parts = []
        for j in range(count):
            low, high = max(first, j * rows), min(first + 256, (j + 1) * rows)
            if low < high:
                parts.append(grad_refs[j][low - j * rows : high - j * rows])
        turned[:, first : first + 256] = jnp.concatenate(parts).T
    for first in range(0, features, step):
        columns = slice(first, first + step)
        for j in range(count):
            held[j * rows : (j + 1) * rows] = block_refs[j][:rows, columns]
        for part, out_ref in enumerate((own_ref, theirs_ref)):
            out_ref[:, columns] = jnp.dot(
                turned[part * tokens : (part + 1) * tokens],
                held[...],
                preferred_element_type=jnp.float32,
            ).astype(out_ref.dtype)


def input_grads(rows, tokens, grads, blocks):
    features = blocks[0].shape[1]
    low = blocks[0].dtype
    count = len(blocks)
    return local_call(
        partial(input_kernel, rows, count),
        (jax.ShapeDtypeStruct((tokens, features), low),) * 2,
        (
            jax.ShapeDtypeStruct((NC * tokens, count * rows), low),
            jax.ShapeDtypeStruct((count * rows, 512), low),
        ),
    )(*grads, *blocks)


def add_kernel(first_ref, second_ref, out_ref):
    total = first_ref[...].astype(jnp.float32) + second_ref[...].astype(jnp.float32)
    out_ref[...] = total.astype(out_ref.dtype)


def added(first, second):
    return local_call(add_kernel, (jax.ShapeDtypeStruct(first.shape, first.dtype),))(first, second)[0]


def plus(first, *others):
    total = first.astype(jnp.float32)
    for one in others:
        total = total + one.astype(jnp.float32)
    return total


def shards(
    attention,
    upstream,
    step_index,
    weight,
    weight_momentum,
    weight_variance,
    norm_gain,
    gain_momentum,
    gain_variance,
):
    rows, features = weight.shape[1:]
    tokens, width = upstream.shape[1:]
    half = rows // 2
    low = jnp.bfloat16
    index = lax.axis_index("fsdp")
    core = index % NC
    x = index // NC % NX
    y = index // (NC * NX)

    gain_row = jnp.pad(norm_gain, ((0, 0), (0, features - rows)))
    own_top, own_bottom, own = packed_rows(weight[0], gain_row)
    below_top = move(own_top, dy=1)
    above_bottom = move(own_bottom, dy=-1)
    below_bottom = move(own_bottom, dy=1)
    above_top = move(own_top, dy=-1)
    across = move(own, dx=1)

    chips = jnp.arange(NY * NX)
    away = (chips // NX - y) % NY * NX + (chips % NX - x) % NX
    order = [0] * (NY * NX)
    for k, (dy, dx) in enumerate(OFFSETS):
        order[dy % NY * NX + dx] = k
    slots = jnp.concatenate(
        [core[None], jnp.array(order, jnp.int32)[away]]
    ).astype(jnp.int32)
    mine, theirs = turned_blocks(upstream[0], rows, slots)

    below_top, above_bottom, mine, theirs = tied(below_top, above_bottom, mine, theirs)
    far_top = move(below_top, dy=1)
    far_bottom = move(above_bottom, dy=-1)
    below, above = stacked_halves((below_top, below_bottom), (above_top, above_bottom))

    far_top, far_bottom, below, above, across = tied(far_top, far_bottom, below, above, across)
    far = jnp.concatenate([far_top, far_bottom])
    across_below = move(across, dy=1)
    across_above = move(across, dy=-1)
    across_far = move(far, dx=1)
    attention_own, theirs, _ = tied(attention[0], theirs, across)
    attn_other = move(attention_own, dcore=1)
    given = move(theirs, dcore=1)
    attn, attn_turned = joined_tokens(attention_own, attn_other)
    outs = [None] * 8
    sums = [None] * 8

    def run(k, block, cost=NO_COST):
        outs[k], sums[k] = forward_block(k, rows, block, attn_turned, mine, given, cost)

    for k, block in [(0, own), (1, across), (2, below), (3, above), (6, far)]:
        run(k, block)
    across_below, across_above, *outs[:4], outs[6] = tied(
        across_below, across_above, *outs[:4], outs[6]
    )
    for k, block in [(4, across_below), (5, across_above)]:
        run(k, block, SMALL_COST)
    across_far, *outs[4:6] = tied(across_far, *outs[4:6])
    run(7, across_far)
    blocks = [own, across, below, above, across_below, across_above, far, across_far]
    sums = sum(sums[1:], sums[0])
    other_sums = move(sums, dcore=1)

    left, right = slice(0, CUT), slice(CUT, features)
    grads = [None] * 8
    gain_parts = [None] * 8

    def run_weight(k, *cuts):
        grads[k], gain_parts[k], terms = weight_block(
            k, rows, width, cuts, sums, other_sums, mine, given, attn, outs[k], blocks[k]
        )
        return terms

    own_across_below = run_weight(4)
    from_above = move(own_across_below[0], dy=-1)
    own_across_above = run_weight(5)
    from_below = move(own_across_above[0], dy=1)
    grads[4], grads[5], outs[7] = tied(grads[4], grads[5], outs[7])
    own_across_far = run_weight(7)
    across_far = move(own_across_far[0], dx=1)
    sums, grads[7], grads[4], grads[5] = tied(sums, grads[7], grads[4], grads[5])
    middle = features // 2
    far_left, far_right = run_weight(6, middle)
    (own_across,) = run_weight(1)
    below_left, below_middle, below_right = run_weight(2, CUT, middle)
    above_left, above_middle, above_right = run_weight(3, CUT, middle)
    own_left, own_right = run_weight(0, CUT)
    gain_own, gain_across, gain_below, gain_above, *gain_rest = gain_parts
    gain_moved = move(jnp.stack([gain_rest[2], gain_rest[3], gain_below, gain_rest[0]]), dy=2)
    input_own, input_theirs = input_grads(rows, tokens, grads, blocks)
    across_far, from_above, from_below, gain_moved, input_theirs = tied(
        across_far, from_above, from_below, gain_moved, input_theirs
    )

    far_down = move(plus(far_left, across_far[:, :middle]).astype(low), dy=-1)
    far_up = move(plus(far_right, across_far[:, middle:]).astype(low), dy=1)
    side = move(plus(own_across, from_above, from_below).astype(low), dx=1)
    gain_up = jnp.stack([gain_above, gain_rest[1]]) + gain_moved[2:]
    gain_up = move(gain_up, dy=1)
    input_given = move(input_theirs, dcore=1)
    grad_input = added(input_own, input_given)
    far_down, far_up, gain_up, grad_input, above_left, below_right = tied(
        far_down, far_up, gain_up, grad_input, above_left, below_right
    )
    downs = [
        plus(below_left, far_down[:, :CUT]).astype(low),
        jnp.concatenate([plus(below_middle, far_down[:, CUT:]).astype(low), below_right], 1),
    ]
    ups = [
        above_left,
        jnp.concatenate([above_middle, plus(above_right, far_up).astype(low)], 1),
    ]
    downs = [move(part, dy=-1) for part in downs]
    ups = [move(part, dy=1) for part in ups]
    gain_pair = jnp.stack([gain_own, gain_across]) + gain_moved[:2] + gain_up
    side, downs[0], ups[0], gain_pair = tied(side, downs[0], ups[0], gain_pair)
    gain_side = move(gain_pair[1], dx=1)
    (grad_left,) = tied(plus(own_left, side[:, left], downs[0], ups[0]))
    local_left = adam_update(
        weight[0, :, left],
        grad_left,
        weight_momentum[0, :, left],
        weight_variance[0, :, left],
        step_index,
    )[0]
    (peer_left,) = swapped((local_left.astype(low),), step_index)
    downs, ups, gain_side, peer_left = tied(downs, ups, gain_side, peer_left)
    local_gain, new_gain_momentum, new_gain_variance = adam_update(
        norm_gain, (gain_pair[0] + gain_side)[None], gain_momentum, gain_variance, step_index
    )
    grad_weight = jnp.concatenate(
        [
            grad_left,
            plus(own_right, side[:, right], downs[1], ups[1]),
        ],
        1,
    )[None]
    local_weight, new_weight_momentum, new_weight_variance = adam_update(
        weight, grad_weight, weight_momentum, weight_variance, step_index
    )
    peer_right, peer_gain = swapped((local_weight[0, :, right].astype(low), local_gain), step_index)
    peer_weight = jnp.concatenate([peer_left, peer_right], 1)[None]
    new_weight = 0.5 * plus(local_weight, peer_weight)
    new_gain = 0.5 * (local_gain + peer_gain)
    return (
        grad_input[None],
        new_weight,
        new_weight_momentum,
        new_weight_variance,
        new_gain,
        new_gain_momentum,
        new_gain_variance,
    )


def solution(mesh):
    block = P("replica", "fsdp", None)
    vector = P("replica", "fsdp")
    return jax.shard_map(
        shards,
        mesh=mesh,
        in_specs=(block, block, P(), block, block, block, vector, vector, vector),
        out_specs=(block, block, block, block, vector, vector, vector),
        check_vma=False,
    )
```

```python
from functools import partial

import jax
import jax.numpy as jnp
from jax import lax
from jax.experimental import pallas as pl
from jax.experimental.pallas import tpu as pltpu
from jax.sharding import PartitionSpec as P

learn_rate = 0.001
beta_first = 0.9
beta_second = 0.999
decay_rate = 0.1
adam_eps = 1e-08
norm_eps = 1e-06

NY, NX, NC = 4, 2, 2
CUT = 768
GAIN_ROWS = 8
EXTRA_BYTES = 0
NO_COST = pl.CostEstimate(flops=0, bytes_accessed=0, transcendentals=0)
SMALL_COST = pl.CostEstimate(flops=1_200_000_000, bytes_accessed=0, transcendentals=0)


def place(y, x, core):
    return ((y % NY) * NX + x % NX) * NC + core % NC


def route(dy, dx, dcore):
    return [
        (place(y, x, core), place(y + dy, x + dx, core + dcore))
        for y in range(NY)
        for x in range(NX)
        for core in range(NC)
    ]


def move(block, dy=0, dx=0, dcore=0):
    return lax.ppermute(block, "fsdp", route(dy, dx, dcore))


def swapped(values, step_index):
    count = lax.axis_size("replica")
    levels = count.bit_length() - 1

    def swap(level, *parts):
        pairs = [(low, low ^ (1 << level)) for low in range(count)]
        return tuple(lax.ppermute(part, "replica", pairs) for part in parts)

    return lax.switch(
        step_index % levels, [partial(swap, level) for level in range(levels)], *values
    )


def adam_update(params, grads, momentum, variance, step_index):
    counted = (step_index + 1).astype(jnp.float32)
    new_momentum = beta_first * momentum + (1.0 - beta_first) * grads
    new_variance = beta_second * variance + (1.0 - beta_second) * grads * grads
    first_hat = new_momentum / (1.0 - jnp.power(jnp.float32(beta_first), counted))
    second_hat = new_variance / (1.0 - jnp.power(jnp.float32(beta_second), counted))
    update = learn_rate * (first_hat / (jnp.sqrt(second_hat) + adam_eps) + decay_rate * params)
    return (params - update, new_momentum, new_variance)


OFFSETS = [(0, 0), (0, 1), (-1, 0), (1, 0), (-1, 1), (1, 1), (2, 0), (2, 1)]


def tied(*values):
    return lax.optimization_barrier(values)


def turn_kernel(rows, slots_ref, up_ref, mine_ref, theirs_ref):
    core = slots_ref[0]
    for chip in range(NY * NX):
        for side in range(NC):
            first = (chip * NC + side) * rows
            left = first // 128 * 128
            right = -(-(first + rows) // 128) * 128
            turned = up_ref[:, left:right].T[first - left : first - left + rows]

            @pl.when(core == side)
            def _():
                mine_ref[slots_ref[1 + chip]] = turned

            @pl.when(core != side)
            def _():
                theirs_ref[slots_ref[1 + chip]] = turned


def turned_blocks(upstream, rows, slots):
    tokens, width = upstream.shape
    shape = jax.ShapeDtypeStruct((NY * NX, rows, tokens), upstream.dtype)
    return pl.pallas_call(
        partial(turn_kernel, rows),
        out_shape=(shape, shape),
        in_specs=[
            pl.BlockSpec(memory_space=pltpu.SMEM),
            pl.BlockSpec(memory_space=pltpu.VMEM),
        ],
        out_specs=(
            pl.BlockSpec(memory_space=pltpu.VMEM),
            pl.BlockSpec(memory_space=pltpu.VMEM),
        ),
        compiler_params=pltpu.CompilerParams(
            vmem_limit_bytes=vmem_limit(upstream, shape, shape)
        ),
        cost_estimate=NO_COST,
    )(slots, upstream)


def vmem_limit(*arrays):
    total = 0
    for array in arrays:
        *outer, above, last = (1,) + tuple(array.shape)
        held = -(-above // 16) * 16 * -(-last // 128) * 128
        for size in outer:
            held *= size
        total += held * jnp.dtype(array.dtype).itemsize
    return total + (4 << 20)


def local_call(kernel, out_shape, scratch=(), cost=NO_COST):
    whole = pl.BlockSpec(memory_space=pltpu.VMEM)

    def call(*operands):
        return pl.pallas_call(
            kernel,
            out_shape=out_shape,
            in_specs=[whole] * len(operands),
            out_specs=jax.tree.map(lambda _: whole, out_shape),
            scratch_shapes=[pltpu.VMEM(held.shape, held.dtype) for held in scratch],
            compiler_params=pltpu.CompilerParams(
                vmem_limit_bytes=vmem_limit(*out_shape, *scratch) + EXTRA_BYTES
            ),
            cost_estimate=cost,
        )(*operands)

    return call


def stack_kernel(count, *refs):
    for pair, out_ref in zip(zip(refs[: 2 * count : 2], refs[1 : 2 * count : 2]), refs[2 * count :]):
        first = 0
        for ref in pair:
            out_ref[first : first + ref.shape[0]] = ref[...]
            first += ref.shape[0]


def stacked_halves(*pairs):
    shape = [
        jax.ShapeDtypeStruct((top.shape[0] + bottom.shape[0], top.shape[1]), top.dtype)
        for top, bottom in pairs
    ]
    flat = [half for pair in pairs for half in pair]
    return local_call(partial(stack_kernel, len(pairs)), tuple(shape), cost=SMALL_COST)(*flat)


def pack_kernel(weight_ref, gain_ref, top_ref, bottom_ref, whole_ref):
    half = top_ref.shape[0]
    rows, features = weight_ref.shape
    low = whole_ref.dtype
    top = weight_ref[:half].astype(low)
    bottom = weight_ref[half:].astype(low)
    gain = jnp.broadcast_to(gain_ref[...], (GAIN_ROWS, features)).astype(low)
    top_ref[...] = top
    bottom_ref[: rows - half] = bottom
    bottom_ref[rows - half :] = gain
    whole_ref[:half] = top
    whole_ref[half:rows] = bottom
    whole_ref[rows:] = gain


def packed_rows(weight, gain_row):
    rows, features = weight.shape
    half = rows // 2
    return local_call(
        pack_kernel,
        tuple(
            jax.ShapeDtypeStruct((count, features), jnp.bfloat16)
            for count in (half, rows - half + GAIN_ROWS, rows + GAIN_ROWS)
        ),
    )(weight, gain_row)


def join_kernel(own_ref, other_ref, joined_ref, turned_ref):
    tokens, features = own_ref.shape
    for part, ref in enumerate((own_ref, other_ref)):
        at = slice(part * tokens, (part + 1) * tokens)
        joined_ref[at] = ref[...]
        for first in range(0, features, 256):
            turned_ref[first : first + 256, at] = ref[:, first : first + 256].T


def joined_tokens(own, other):
    tokens, features = own.shape
    return local_call(
        join_kernel,
        (
            jax.ShapeDtypeStruct((NC * tokens, features), own.dtype),
            jax.ShapeDtypeStruct((features, NC * tokens), own.dtype),
        ),
    )(own, other)


def gain_column(block_ref, rows):
    wide = -(-rows // 128) * 128
    return block_ref[rows : rows + GAIN_ROWS, :wide].astype(jnp.float32).T[:rows, :1]


def forward_kernel(k, rows, block_ref, attn_ref, mine_ref, given_ref, out_ref, stat_ref):
    tokens = mine_ref.shape[2]
    gain = gain_column(block_ref, rows)
    for part, up_ref in enumerate((mine_ref, given_ref)):
        at = slice(part * tokens, (part + 1) * tokens)
        out = jnp.dot(block_ref[:rows], attn_ref[:, at], preferred_element_type=jnp.float32)
        out_ref[:, at] = out
        scaled = up_ref[k].astype(jnp.float32) * gain
        stat_ref[0:1, at] = jnp.sum(out * out, 0, keepdims=True)
        stat_ref[1:2, at] = jnp.sum(out * scaled, 0, keepdims=True)


def forward_block(k, rows, block, attn, mine, given, cost):
    count = attn.shape[1]
    return local_call(
        partial(forward_kernel, k, rows),
        (
            jax.ShapeDtypeStruct((rows, count), jnp.float32),
            jax.ShapeDtypeStruct((2, count), jnp.float32),
        ),
        cost=cost,
    )(block, attn, mine, given)


def weight_kernel(k, rows, width, *refs):
    sums_ref, other_sums_ref, mine_ref, given_ref, attn_ref, out_ref, block_ref = refs[:7]
    grad_ref, gain_ref = refs[7:9]
    term_refs = refs[9:]
    tokens = mine_ref.shape[2]
    gain = gain_column(block_ref, rows)
    folded = jnp.zeros((rows, 128), jnp.float32)
    for part, up_ref in enumerate((mine_ref, given_ref)):
        here = slice(part * tokens, (part + 1) * tokens)
        there = slice((1 - part) * tokens, (2 - part) * tokens)
        inverse_row = lax.rsqrt(
            (sums_ref[0:1, here] + other_sums_ref[0:1, there]) / width + norm_eps
        )
        slope_row = (sums_ref[1:2, here] + other_sums_ref[1:2, there]) / width
        slope_row = slope_row * inverse_row * inverse_row
        for first in range(0, tokens, 128):
            inverse = inverse_row[:, first : first + 128]
            slope = slope_row[:, first : first + 128]
            at = slice(part * tokens + first, part * tokens + first + 128)
            out = out_ref[:, at]
            up = up_ref[k, :, first : first + 128].astype(jnp.float32)
            grad = inverse * (up * gain - out * slope)
            grad_ref[:, at] = grad.astype(grad_ref.dtype)
            folded = folded + up * (out * inverse)
    gain_ref[...] = jnp.sum(folded.T, 0, keepdims=True)
    begin = 0
    for term_ref in term_refs:
        for first in range(0, term_ref.shape[1], 256):
            columns = slice(begin + first, begin + first + 256)
            term_ref[:, first : first + 256] = jnp.dot(
                grad_ref[...], attn_ref[:, columns], preferred_element_type=jnp.float32
            ).astype(term_ref.dtype)
        begin += term_ref.shape[1]


def weight_block(k, rows, width, cuts, sums, other_sums, mine, given, attn, out, block):
    tokens, features = attn.shape
    edges = (0,) + cuts + (features,)
    got = local_call(
        partial(weight_kernel, k, rows, width),
        (
            jax.ShapeDtypeStruct((rows, tokens), mine.dtype),
            jax.ShapeDtypeStruct((1, rows), jnp.float32),
        )
        + tuple(
            jax.ShapeDtypeStruct((rows, end - begin), mine.dtype)
            for begin, end in zip(edges, edges[1:])
        ),
    )(sums, other_sums, mine, given, attn, out, block)
    return got[0], got[1][0], got[2:]


def input_kernel(rows, count, *refs):
    grad_refs, block_refs = refs[:count], refs[count : 2 * count]
    own_ref, theirs_ref, turned, held = refs[2 * count :]
    tokens, features = own_ref.shape
    step = held.shape[1]
    for first in range(0, count * rows, 256):
        parts = []
        for j in range(count):
            low, high = max(first, j * rows), min(first + 256, (j + 1) * rows)
            if low < high:
                parts.append(grad_refs[j][low - j * rows : high - j * rows])
        turned[:, first : first + 256] = jnp.concatenate(parts).T
    for first in range(0, features, step):
        columns = slice(first, first + step)
        for j in range(count):
            held[j * rows : (j + 1) * rows] = block_refs[j][:rows, columns]
        for part, out_ref in enumerate((own_ref, theirs_ref)):
            out_ref[:, columns] = jnp.dot(
                turned[part * tokens : (part + 1) * tokens],
                held[...],
                preferred_element_type=jnp.float32,
            ).astype(out_ref.dtype)


def input_grads(rows, tokens, grads, blocks):
    features = blocks[0].shape[1]
    low = blocks[0].dtype
    count = len(blocks)
    return local_call(
        partial(input_kernel, rows, count),
        (jax.ShapeDtypeStruct((tokens, features), low),) * 2,
        (
            jax.ShapeDtypeStruct((NC * tokens, count * rows), low),
            jax.ShapeDtypeStruct((count * rows, 512), low),
        ),
    )(*grads, *blocks)


def add_kernel(first_ref, second_ref, out_ref):
    total = first_ref[...].astype(jnp.float32) + second_ref[...].astype(jnp.float32)
    out_ref[...] = total.astype(out_ref.dtype)


def added(first, second):
    return local_call(add_kernel, (jax.ShapeDtypeStruct(first.shape, first.dtype),))(first, second)[0]


def plus(first, *others):
    total = first.astype(jnp.float32)
    for one in others:
        total = total + one.astype(jnp.float32)
    return total


def shards(
    attention,
    upstream,
    step_index,
    weight,
    weight_momentum,
    weight_variance,
    norm_gain,
    gain_momentum,
    gain_variance,
):
    rows, features = weight.shape[1:]
    tokens, width = upstream.shape[1:]
    half = rows // 2
    low = jnp.bfloat16
    index = lax.axis_index("fsdp")
    core = index % NC
    x = index // NC % NX
    y = index // (NC * NX)

    gain_row = jnp.pad(norm_gain, ((0, 0), (0, features - rows)))
    own_top, own_bottom, own = packed_rows(weight[0], gain_row)
    below_top = move(own_top, dy=1)
    above_bottom = move(own_bottom, dy=-1)
    below_bottom = move(own_bottom, dy=1)
    above_top = move(own_top, dy=-1)
    across = move(own, dx=1)

    chips = jnp.arange(NY * NX)
    away = (chips // NX - y) % NY * NX + (chips % NX - x) % NX
    order = [0] * (NY * NX)
    for k, (dy, dx) in enumerate(OFFSETS):
        order[dy % NY * NX + dx] = k
    slots = jnp.concatenate(
        [core[None], jnp.array(order, jnp.int32)[away]]
    ).astype(jnp.int32)
    mine, theirs = turned_blocks(upstream[0], rows, slots)

    below_top, above_bottom, mine, theirs = tied(below_top, above_bottom, mine, theirs)
    far_top = move(below_top, dy=1)
    far_bottom = move(above_bottom, dy=-1)
    below, above = stacked_halves((below_top, below_bottom), (above_top, above_bottom))

    far_top, far_bottom, below, above, across = tied(far_top, far_bottom, below, above, across)
    far = jnp.concatenate([far_top, far_bottom])
    across_below = move(across, dy=1)
    across_above = move(across, dy=-1)
    across_far = move(far, dx=1)
    attention_own, theirs, _ = tied(attention[0], theirs, across)
    attn_other = move(attention_own, dcore=1)
    given = move(theirs, dcore=1)
    attn, attn_turned = joined_tokens(attention_own, attn_other)
    outs = [None] * 8
    sums = [None] * 8

    def run(k, block, cost=NO_COST):
        outs[k], sums[k] = forward_block(k, rows, block, attn_turned, mine, given, cost)

    for k, block in [(0, own), (1, across), (2, below), (3, above), (6, far)]:
        run(k, block)
    across_below, across_above, *outs[:4], outs[6] = tied(
        across_below, across_above, *outs[:4], outs[6]
    )
    for k, block in [(4, across_below), (5, across_above)]:
        run(k, block, SMALL_COST)
    across_far, *outs[4:6] = tied(across_far, *outs[4:6])
    run(7, across_far)
    blocks = [own, across, below, above, across_below, across_above, far, across_far]
    sums = sum(sums[1:], sums[0])
    other_sums = move(sums, dcore=1)

    left, right = slice(0, CUT), slice(CUT, features)
    grads = [None] * 8
    gain_parts = [None] * 8

    def run_weight(k, *cuts):
        grads[k], gain_parts[k], terms = weight_block(
            k, rows, width, cuts, sums, other_sums, mine, given, attn, outs[k], blocks[k]
        )
        return terms

    own_across_below = run_weight(4)
    from_above = move(own_across_below[0], dy=-1)
    own_across_above = run_weight(5)
    from_below = move(own_across_above[0], dy=1)
    grads[4], grads[5], outs[7] = tied(grads[4], grads[5], outs[7])
    own_across_far = run_weight(7)
    across_far = move(own_across_far[0], dx=1)
    sums, grads[7], grads[4], grads[5] = tied(sums, grads[7], grads[4], grads[5])
    middle = features // 2
    far_left, far_right = run_weight(6, middle)
    (own_across,) = run_weight(1)
    below_left, below_middle, below_right = run_weight(2, CUT, middle)
    above_left, above_middle, above_right = run_weight(3, CUT, middle)
    own_left, own_right = run_weight(0, CUT)
    gain_own, gain_across, gain_below, gain_above, *gain_rest = gain_parts
    gain_moved = move(jnp.stack([gain_rest[2], gain_rest[3], gain_below, gain_rest[0]]), dy=2)
    input_own, input_theirs = input_grads(rows, tokens, grads, blocks)
    across_far, from_above, from_below, gain_moved, input_theirs = tied(
        across_far, from_above, from_below, gain_moved, input_theirs
    )

    side_sum = plus(own_across, from_above, from_below).astype(low)
    across_far, side_sum = tied(across_far, side_sum)
    side = move(side_sum, dx=1)
    far_down = move(plus(far_left, across_far[:, :middle]).astype(low), dy=-1)
    far_up = move(plus(far_right, across_far[:, middle:]).astype(low), dy=1)
    gain_up = jnp.stack([gain_above, gain_rest[1]]) + gain_moved[2:]
    gain_up = move(gain_up, dy=1)
    input_given = move(input_theirs, dcore=1)
    grad_input = added(input_own, input_given)
    far_down, far_up, gain_up, grad_input, above_left, below_right = tied(
        far_down, far_up, gain_up, grad_input, above_left, below_right
    )
    downs = [
        plus(below_left, far_down[:, :CUT]).astype(low),
        jnp.concatenate([plus(below_middle, far_down[:, CUT:]).astype(low), below_right], 1),
    ]
    ups = [
        above_left,
        jnp.concatenate([above_middle, plus(above_right, far_up).astype(low)], 1),
    ]
    downs = [move(part, dy=-1) for part in downs]
    ups = [move(part, dy=1) for part in ups]
    gain_pair = jnp.stack([gain_own, gain_across]) + gain_moved[:2] + gain_up
    side, downs[0], ups[0], gain_pair = tied(side, downs[0], ups[0], gain_pair)
    gain_side = move(gain_pair[1], dx=1)
    (grad_left,) = tied(plus(own_left, side[:, left], downs[0], ups[0]))
    local_left = adam_update(
        weight[0, :, left],
        grad_left,
        weight_momentum[0, :, left],
        weight_variance[0, :, left],
        step_index,
    )[0]
    (peer_left,) = swapped((local_left.astype(low),), step_index)
    downs, ups, gain_side, peer_left = tied(downs, ups, gain_side, peer_left)
    local_gain, new_gain_momentum, new_gain_variance = adam_update(
        norm_gain, (gain_pair[0] + gain_side)[None], gain_momentum, gain_variance, step_index
    )
    grad_weight = jnp.concatenate(
        [
            grad_left,
            plus(own_right, side[:, right], downs[1], ups[1]),
        ],
        1,
    )[None]
    local_weight, new_weight_momentum, new_weight_variance = adam_update(
        weight, grad_weight, weight_momentum, weight_variance, step_index
    )
    peer_right, peer_gain = swapped((local_weight[0, :, right].astype(low), local_gain), step_index)
    peer_weight = jnp.concatenate([peer_left, peer_right], 1)[None]
    new_weight = 0.5 * plus(local_weight, peer_weight)
    new_gain = 0.5 * (local_gain + peer_gain)
    return (
        grad_input[None],
        new_weight,
        new_weight_momentum,
        new_weight_variance,
        new_gain,
        new_gain_momentum,
        new_gain_variance,
    )


def solution(mesh):
    block = P("replica", "fsdp", None)
    vector = P("replica", "fsdp")
    return jax.shard_map(
        shards,
        mesh=mesh,
        in_specs=(block, block, P(), block, block, block, vector, vector, vector),
        out_specs=(block, block, block, block, vector, vector, vector),
        check_vma=False,
    )
```

```python
from functools import partial

import jax
import jax.numpy as jnp
from jax import lax
from jax.experimental import pallas as pl
from jax.experimental.pallas import tpu as pltpu
from jax.sharding import PartitionSpec as P

learn_rate = 0.001
beta_first = 0.9
beta_second = 0.999
decay_rate = 0.1
adam_eps = 1e-08
norm_eps = 1e-06

NY, NX, NC = 4, 2, 2
CUT = 768
GAIN_ROWS = 8
EXTRA_BYTES = 0
NO_COST = pl.CostEstimate(flops=0, bytes_accessed=0, transcendentals=0)
SMALL_COST = pl.CostEstimate(flops=1_200_000_000, bytes_accessed=0, transcendentals=0)


def place(y, x, core):
    return ((y % NY) * NX + x % NX) * NC + core % NC


def route(dy, dx, dcore):
    return [
        (place(y, x, core), place(y + dy, x + dx, core + dcore))
        for y in range(NY)
        for x in range(NX)
        for core in range(NC)
    ]


def move(block, dy=0, dx=0, dcore=0):
    return lax.ppermute(block, "fsdp", route(dy, dx, dcore))


def swapped(values, step_index):
    count = lax.axis_size("replica")
    levels = count.bit_length() - 1

    def swap(level, *parts):
        pairs = [(low, low ^ (1 << level)) for low in range(count)]
        return tuple(lax.ppermute(part, "replica", pairs) for part in parts)

    return lax.switch(
        step_index % levels, [partial(swap, level) for level in range(levels)], *values
    )


def adam_update(params, grads, momentum, variance, step_index):
    counted = (step_index + 1).astype(jnp.float32)
    new_momentum = beta_first * momentum + (1.0 - beta_first) * grads
    new_variance = beta_second * variance + (1.0 - beta_second) * grads * grads
    first_hat = new_momentum / (1.0 - jnp.power(jnp.float32(beta_first), counted))
    second_hat = new_variance / (1.0 - jnp.power(jnp.float32(beta_second), counted))
    update = learn_rate * (first_hat / (jnp.sqrt(second_hat) + adam_eps) + decay_rate * params)
    return (params - update, new_momentum, new_variance)


OFFSETS = [(0, 0), (0, 1), (-1, 0), (1, 0), (-1, 1), (1, 1), (2, 0), (2, 1)]


def tied(*values):
    return lax.optimization_barrier(values)


def turn_kernel(rows, slots_ref, up_ref, mine_ref, theirs_ref):
    core = slots_ref[0]
    for chip in range(NY * NX):
        for side in range(NC):
            first = (chip * NC + side) * rows
            left = first // 128 * 128
            right = -(-(first + rows) // 128) * 128
            turned = up_ref[:, left:right].T[first - left : first - left + rows]

            @pl.when(core == side)
            def _():
                mine_ref[slots_ref[1 + chip]] = turned

            @pl.when(core != side)
            def _():
                theirs_ref[slots_ref[1 + chip]] = turned


def turned_blocks(upstream, rows, slots):
    tokens, width = upstream.shape
    shape = jax.ShapeDtypeStruct((NY * NX, rows, tokens), upstream.dtype)
    return pl.pallas_call(
        partial(turn_kernel, rows),
        out_shape=(shape, shape),
        in_specs=[
            pl.BlockSpec(memory_space=pltpu.SMEM),
            pl.BlockSpec(memory_space=pltpu.VMEM),
        ],
        out_specs=(
            pl.BlockSpec(memory_space=pltpu.VMEM),
            pl.BlockSpec(memory_space=pltpu.VMEM),
        ),
        compiler_params=pltpu.CompilerParams(
            vmem_limit_bytes=vmem_limit(upstream, shape, shape)
        ),
        cost_estimate=NO_COST,
    )(slots, upstream)


def vmem_limit(*arrays):
    total = 0
    for array in arrays:
        *outer, above, last = (1,) + tuple(array.shape)
        held = -(-above // 16) * 16 * -(-last // 128) * 128
        for size in outer:
            held *= size
        total += held * jnp.dtype(array.dtype).itemsize
    return total + (4 << 20)


def local_call(kernel, out_shape, scratch=(), cost=NO_COST):
    whole = pl.BlockSpec(memory_space=pltpu.VMEM)

    def call(*operands):
        return pl.pallas_call(
            kernel,
            out_shape=out_shape,
            in_specs=[whole] * len(operands),
            out_specs=jax.tree.map(lambda _: whole, out_shape),
            scratch_shapes=[pltpu.VMEM(held.shape, held.dtype) for held in scratch],
            compiler_params=pltpu.CompilerParams(
                vmem_limit_bytes=vmem_limit(*out_shape, *scratch) + EXTRA_BYTES
            ),
            cost_estimate=cost,
        )(*operands)

    return call


def stack_kernel(count, *refs):
    for pair, out_ref in zip(zip(refs[: 2 * count : 2], refs[1 : 2 * count : 2]), refs[2 * count :]):
        first = 0
        for ref in pair:
            out_ref[first : first + ref.shape[0]] = ref[...]
            first += ref.shape[0]


def stacked_halves(*pairs):
    shape = [
        jax.ShapeDtypeStruct((top.shape[0] + bottom.shape[0], top.shape[1]), top.dtype)
        for top, bottom in pairs
    ]
    flat = [half for pair in pairs for half in pair]
    return local_call(partial(stack_kernel, len(pairs)), tuple(shape), cost=SMALL_COST)(*flat)


def pack_kernel(weight_ref, gain_ref, top_ref, bottom_ref, whole_ref):
    half = top_ref.shape[0]
    rows, features = weight_ref.shape
    low = whole_ref.dtype
    top = weight_ref[:half].astype(low)
    bottom = weight_ref[half:].astype(low)
    gain = jnp.broadcast_to(gain_ref[...], (GAIN_ROWS, features)).astype(low)
    top_ref[...] = top
    bottom_ref[: rows - half] = bottom
    bottom_ref[rows - half :] = gain
    whole_ref[:half] = top
    whole_ref[half:rows] = bottom
    whole_ref[rows:] = gain


def packed_rows(weight, gain_row):
    rows, features = weight.shape
    half = rows // 2
    return local_call(
        pack_kernel,
        tuple(
            jax.ShapeDtypeStruct((count, features), jnp.bfloat16)
            for count in (half, rows - half + GAIN_ROWS, rows + GAIN_ROWS)
        ),
    )(weight, gain_row)


def join_kernel(own_ref, other_ref, joined_ref, turned_ref):
    tokens, features = own_ref.shape
    for part, ref in enumerate((own_ref, other_ref)):
        at = slice(part * tokens, (part + 1) * tokens)
        joined_ref[at] = ref[...]
        for first in range(0, features, 256):
            turned_ref[first : first + 256, at] = ref[:, first : first + 256].T


def joined_tokens(own, other):
    tokens, features = own.shape
    return local_call(
        join_kernel,
        (
            jax.ShapeDtypeStruct((NC * tokens, features), own.dtype),
            jax.ShapeDtypeStruct((features, NC * tokens), own.dtype),
        ),
    )(own, other)


def gain_column(block_ref, rows):
    wide = -(-rows // 128) * 128
    return block_ref[rows : rows + GAIN_ROWS, :wide].astype(jnp.float32).T[:rows, :1]


def forward_kernel(k, rows, block_ref, attn_ref, mine_ref, given_ref, out_ref, stat_ref):
    tokens = mine_ref.shape[2]
    gain = gain_column(block_ref, rows)
    for part, up_ref in enumerate((mine_ref, given_ref)):
        at = slice(part * tokens, (part + 1) * tokens)
        out = jnp.dot(block_ref[:rows], attn_ref[:, at], preferred_element_type=jnp.float32)
        out_ref[:, at] = out
        scaled = up_ref[k].astype(jnp.float32) * gain
        stat_ref[0:1, at] = jnp.sum(out * out, 0, keepdims=True)
        stat_ref[1:2, at] = jnp.sum(out * scaled, 0, keepdims=True)


def forward_block(k, rows, block, attn, mine, given, cost):
    count = attn.shape[1]
    return local_call(
        partial(forward_kernel, k, rows),
        (
            jax.ShapeDtypeStruct((rows, count), jnp.float32),
            jax.ShapeDtypeStruct((2, count), jnp.float32),
        ),
        cost=cost,
    )(block, attn, mine, given)


def weight_kernel(k, rows, width, *refs):
    sums_ref, other_sums_ref, mine_ref, given_ref, attn_ref, out_ref, block_ref = refs[:7]
    grad_ref, gain_ref = refs[7:9]
    term_refs = refs[9:]
    tokens = mine_ref.shape[2]
    gain = gain_column(block_ref, rows)
    folded = jnp.zeros((rows, 128), jnp.float32)
    for part, up_ref in enumerate((mine_ref, given_ref)):
        here = slice(part * tokens, (part + 1) * tokens)
        there = slice((1 - part) * tokens, (2 - part) * tokens)
        inverse_row = lax.rsqrt(
            (sums_ref[0:1, here] + other_sums_ref[0:1, there]) / width + norm_eps
        )
        slope_row = (sums_ref[1:2, here] + other_sums_ref[1:2, there]) / width
        slope_row = slope_row * inverse_row * inverse_row
        for first in range(0, tokens, 128):
            inverse = inverse_row[:, first : first + 128]
            slope = slope_row[:, first : first + 128]
            at = slice(part * tokens + first, part * tokens + first + 128)
            out = out_ref[:, at]
            up = up_ref[k, :, first : first + 128].astype(jnp.float32)
            grad = inverse * (up * gain - out * slope)
            grad_ref[:, at] = grad.astype(grad_ref.dtype)
            folded = folded + up * (out * inverse)
    gain_ref[...] = jnp.sum(folded.T, 0, keepdims=True)
    begin = 0
    for term_ref in term_refs:
        for first in range(0, term_ref.shape[1], 256):
            columns = slice(begin + first, begin + first + 256)
            term_ref[:, first : first + 256] = jnp.dot(
                grad_ref[...], attn_ref[:, columns], preferred_element_type=jnp.float32
            ).astype(term_ref.dtype)
        begin += term_ref.shape[1]


def weight_block(k, rows, width, cuts, sums, other_sums, mine, given, attn, out, block):
    tokens, features = attn.shape
    edges = (0,) + cuts + (features,)
    got = local_call(
        partial(weight_kernel, k, rows, width),
        (
            jax.ShapeDtypeStruct((rows, tokens), mine.dtype),
            jax.ShapeDtypeStruct((1, rows), jnp.float32),
        )
        + tuple(
            jax.ShapeDtypeStruct((rows, end - begin), mine.dtype)
            for begin, end in zip(edges, edges[1:])
        ),
    )(sums, other_sums, mine, given, attn, out, block)
    return got[0], got[1][0], got[2:]


def input_kernel(rows, count, *refs):
    grad_refs, block_refs = refs[:count], refs[count : 2 * count]
    own_ref, theirs_ref, turned, held = refs[2 * count :]
    tokens, features = own_ref.shape
    step = held.shape[1]
    for first in range(0, count * rows, 256):
        parts = []
        for j in range(count):
            low, high = max(first, j * rows), min(first + 256, (j + 1) * rows)
            if low < high:
                parts.append(grad_refs[j][low - j * rows : high - j * rows])
        turned[:, first : first + 256] = jnp.concatenate(parts).T
    for first in range(0, features, step):
        columns = slice(first, first + step)
        for j in range(count):
            held[j * rows : (j + 1) * rows] = block_refs[j][:rows, columns]
        for part, out_ref in enumerate((own_ref, theirs_ref)):
            out_ref[:, columns] = jnp.dot(
                turned[part * tokens : (part + 1) * tokens],
                held[...],
                preferred_element_type=jnp.float32,
            ).astype(out_ref.dtype)


def input_grads(rows, tokens, grads, blocks):
    features = blocks[0].shape[1]
    low = blocks[0].dtype
    count = len(blocks)
    return local_call(
        partial(input_kernel, rows, count),
        (jax.ShapeDtypeStruct((tokens, features), low),) * 2,
        (
            jax.ShapeDtypeStruct((NC * tokens, count * rows), low),
            jax.ShapeDtypeStruct((count * rows, 512), low),
        ),
    )(*grads, *blocks)


def add_kernel(first_ref, second_ref, out_ref):
    total = first_ref[...].astype(jnp.float32) + second_ref[...].astype(jnp.float32)
    out_ref[...] = total.astype(out_ref.dtype)


def added(first, second):
    return local_call(add_kernel, (jax.ShapeDtypeStruct(first.shape, first.dtype),))(first, second)[0]


def plus(first, *others):
    total = first.astype(jnp.float32)
    for one in others:
        total = total + one.astype(jnp.float32)
    return total


def shards(
    attention,
    upstream,
    step_index,
    weight,
    weight_momentum,
    weight_variance,
    norm_gain,
    gain_momentum,
    gain_variance,
):
    rows, features = weight.shape[1:]
    tokens, width = upstream.shape[1:]
    half = rows // 2
    low = jnp.bfloat16
    index = lax.axis_index("fsdp")
    core = index % NC
    x = index // NC % NX
    y = index // (NC * NX)

    gain_row = jnp.pad(norm_gain, ((0, 0), (0, features - rows)))
    own_top, own_bottom, own = packed_rows(weight[0], gain_row)
    below_top = move(own_top, dy=1)
    above_bottom = move(own_bottom, dy=-1)
    below_bottom = move(own_bottom, dy=1)
    above_top = move(own_top, dy=-1)
    across = move(own, dx=1)

    chips = jnp.arange(NY * NX)
    away = (chips // NX - y) % NY * NX + (chips % NX - x) % NX
    order = [0] * (NY * NX)
    for k, (dy, dx) in enumerate(OFFSETS):
        order[dy % NY * NX + dx] = k
    slots = jnp.concatenate(
        [core[None], jnp.array(order, jnp.int32)[away]]
    ).astype(jnp.int32)
    mine, theirs = turned_blocks(upstream[0], rows, slots)

    below_top, above_bottom, mine, theirs = tied(below_top, above_bottom, mine, theirs)
    far_top = move(below_top, dy=1)
    far_bottom = move(above_bottom, dy=-1)
    below, above = stacked_halves((below_top, below_bottom), (above_top, above_bottom))

    far_top, far_bottom, below, above, across = tied(far_top, far_bottom, below, above, across)
    far = jnp.concatenate([far_top, far_bottom])
    across_below = move(across, dy=1)
    across_above = move(across, dy=-1)
    across_far = move(far, dx=1)
    attention_own, theirs, _ = tied(attention[0], theirs, across)
    attn_other = move(attention_own, dcore=1)
    given = move(theirs, dcore=1)
    attn, attn_turned = joined_tokens(attention_own, attn_other)
    outs = [None] * 8
    sums = [None] * 8

    def run(k, block, cost=NO_COST):
        outs[k], sums[k] = forward_block(k, rows, block, attn_turned, mine, given, cost)

    for k, block in [(0, own), (1, across), (2, below), (3, above), (6, far)]:
        run(k, block)
    across_below, across_above, *outs[:4], outs[6] = tied(
        across_below, across_above, *outs[:4], outs[6]
    )
    for k, block in [(4, across_below), (5, across_above)]:
        run(k, block, SMALL_COST)
    across_far, *outs[4:6] = tied(across_far, *outs[4:6])
    run(7, across_far)
    blocks = [own, across, below, above, across_below, across_above, far, across_far]
    sums = sum(sums[1:], sums[0])
    other_sums = move(sums, dcore=1)

    left, right = slice(0, CUT), slice(CUT, features)
    grads = [None] * 8
    gain_parts = [None] * 8

    def run_weight(k, *cuts):
        grads[k], gain_parts[k], terms = weight_block(
            k, rows, width, cuts, sums, other_sums, mine, given, attn, outs[k], blocks[k]
        )
        return terms

    own_across_below = run_weight(4)
    from_above = move(own_across_below[0], dy=-1)
    own_across_above = run_weight(5)
    from_below = move(own_across_above[0], dy=1)
    grads[4], grads[5], outs[7] = tied(grads[4], grads[5], outs[7])
    own_across_far = run_weight(7)
    across_far = move(own_across_far[0], dx=1)
    sums, grads[7], grads[4], grads[5] = tied(sums, grads[7], grads[4], grads[5])
    middle = features // 2
    far_left, far_right = run_weight(6, middle)
    (own_across,) = run_weight(1)
    below_left, below_middle, below_right = run_weight(2, CUT, middle)
    above_left, above_middle, above_right = run_weight(3, CUT, middle)
    own_left, own_right = run_weight(0, CUT)
    gain_own, gain_across, gain_below, gain_above, *gain_rest = gain_parts
    gain_moved = move(jnp.stack([gain_rest[2], gain_rest[3], gain_below, gain_rest[0]]), dy=2)
    input_own, input_theirs = input_grads(rows, tokens, grads, blocks)
    across_far, from_above, from_below, gain_moved, input_theirs = tied(
        across_far, from_above, from_below, gain_moved, input_theirs
    )

    side_sum = plus(own_across, from_above, from_below).astype(low)
    across_far, side_sum = tied(across_far, side_sum)
    side = move(side_sum, dx=1)
    far_down = move(plus(far_left, across_far[:, :middle]).astype(low), dy=-1)
    far_up = move(plus(far_right, across_far[:, middle:]).astype(low), dy=1)
    gain_up = jnp.stack([gain_above, gain_rest[1]]) + gain_moved[2:]
    gain_up = move(gain_up, dy=1)
    input_given = move(input_theirs, dcore=1)
    grad_input = added(input_own, input_given)
    far_down, far_up, grad_input, above_left, below_right = tied(
        far_down, far_up, grad_input, above_left, below_right
    )
    downs = [
        plus(below_left, far_down[:, :CUT]).astype(low),
        jnp.concatenate([plus(below_middle, far_down[:, CUT:]).astype(low), below_right], 1),
    ]
    ups = [
        above_left,
        jnp.concatenate([above_middle, plus(above_right, far_up).astype(low)], 1),
    ]
    downs = [move(part, dy=-1) for part in downs]
    ups = [move(part, dy=1) for part in ups]
    gain_pair = jnp.stack([gain_own, gain_across]) + gain_moved[:2] + gain_up
    side, downs[0], ups[0], gain_pair = tied(side, downs[0], ups[0], gain_pair)
    gain_side = move(gain_pair[1], dx=1)
    (grad_left,) = tied(plus(own_left, side[:, left], downs[0], ups[0]))
    local_left = adam_update(
        weight[0, :, left],
        grad_left,
        weight_momentum[0, :, left],
        weight_variance[0, :, left],
        step_index,
    )[0]
    (peer_left,) = swapped((local_left.astype(low),), step_index)
    downs, ups, gain_side, peer_left = tied(downs, ups, gain_side, peer_left)
    local_gain, new_gain_momentum, new_gain_variance = adam_update(
        norm_gain, (gain_pair[0] + gain_side)[None], gain_momentum, gain_variance, step_index
    )
    grad_weight = jnp.concatenate(
        [
            grad_left,
            plus(own_right, side[:, right], downs[1], ups[1]),
        ],
        1,
    )[None]
    local_weight, new_weight_momentum, new_weight_variance = adam_update(
        weight, grad_weight, weight_momentum, weight_variance, step_index
    )
    peer_right, peer_gain = swapped((local_weight[0, :, right].astype(low), local_gain), step_index)
    peer_weight = jnp.concatenate([peer_left, peer_right], 1)[None]
    new_weight = 0.5 * plus(local_weight, peer_weight)
    new_gain = 0.5 * (local_gain + peer_gain)
    return (
        grad_input[None],
        new_weight,
        new_weight_momentum,
        new_weight_variance,
        new_gain,
        new_gain_momentum,
        new_gain_variance,
    )


def solution(mesh):
    block = P("replica", "fsdp", None)
    vector = P("replica", "fsdp")
    return jax.shard_map(
        shards,
        mesh=mesh,
        in_specs=(block, block, P(), block, block, block, vector, vector, vector),
        out_specs=(block, block, block, block, vector, vector, vector),
        check_vma=False,
    )
```
